256 devices in a mesh: tm: 32 (over y, z_lo, core), head: 8 (over z_hi, x).
Axes of the slice: x: 4, y: 4, z: 8 (z_hi: 2, z_lo: 4; z = z_hi * 4 + z_lo), core: 2. Of those that a mesh axis runs over, the one named last changes fastest.
Arguments:
- latents: bfloat16 [16384, 3072], P(('tm', 'head')), may hold values from -6 to 6
- cotangent: bfloat16 [16384, 3072], P(('tm', 'head')), may hold values from -6 to 6
- norm_gain: float32 [3072], replicated, may hold values from 0.1 to 1.9
- w_qkv: bfloat16 [3072, 3, 3072], P(None, None, 'head'), may hold values from -0.114763592 to 0.114763592
- w_out: bfloat16 [3072, 3072], P('head'), may hold values from -0.109375 to 0.109375
Outputs:
- input_grad: bfloat16 [16384, 3072], P(('tm', 'head'))
The draws below stay inside these ranges and needn't reach their ends.
All inputs are finite; a program needn't handle non-finite values.
Results may differ from the reference program's by a relative error of at most 0.012.
Values may be sent and summed in bfloat16 or wider, within the bound.
A program may use at most 128 MiB of HBM per device.

```python
import jax
import jax.numpy as jnp
from jax import lax

D = 3072
HEADS = 24
HEAD_DIM = 128
FRAME_TOK = 512
TOKENS = 16384
N_TM = 32
N_HEAD = 8


def draw_latents(key, part):
    result = jax.random.truncated_normal(jax.random.fold_in(key, 1), -6.0, 6.0, (TOKENS, D), jnp.float32)
    return result.astype(jnp.bfloat16)


def draw_w_qkv(key, part):
    result = jax.random.truncated_normal(jax.random.fold_in(key, 21), -6.0, 6.0, (D, 3, D), jnp.float32) * D ** (-0.5)
    return result.astype(jnp.bfloat16)


def levels(key, dims, pieces, smallest, high):
    gain = 1.0
    for dim, blocks in pieces:
        steps = jax.random.uniform(jax.random.fold_in(jax.random.fold_in(key, 6), dim), (blocks,), jnp.float32, smallest / len(pieces), high / len(pieces))
        gain = gain * jnp.repeat(jnp.exp(steps), dims[dim] // blocks).reshape((-1,) + (1,) * (len(dims) - 1 - dim))
    return gain


def gaussian(rng, extent, scale, reach, split=(), held_as=jnp.bfloat16):
    loudness = levels(rng, extent, split, -0.22, 0.18) if split else 1.0
    drawn = jax.random.normal(rng, extent, jnp.float32) * scale * loudness
    return jnp.minimum(jnp.maximum(drawn, -reach), reach).astype(held_as)


def setup_inputs(seed: int = 0) -> dict:
    key_list = jax.random.split(jax.random.key(seed), 6)
    latents = draw_latents(jax.random.fold_in(key_list[5], 71), 0)
    cotangent = gaussian(key_list[1], (TOKENS, D), 1.0, 6.0, ((0, 256),))
    norm_gain = jnp.clip(1.0 + 0.18 * jax.random.normal(key_list[2], (D,), jnp.float32), 0.1, 1.9)
    w_qkv = draw_w_qkv(jax.random.fold_in(key_list[5], 71), 0)
    w_out = gaussian(key_list[4], (D, D), D ** -0.5, 0.109375, ((0, 8),))
    return {"latents": latents, "cotangent": cotangent, "norm_gain": norm_gain, "w_qkv": w_qkv, "w_out": w_out}


EPSILON = 1e-06

def round_keep(value):
    return lax.optimization_barrier(value.astype(jnp.bfloat16)).astype(jnp.float32)

def frame_grads(inputs):
    queries, keys_own, keys_prev, values_own, values_prev, grad_attn, has_prev = inputs
    scale = HEAD_DIM ** (-0.5)
    query_f = queries.astype(jnp.float32)
    grad_f = grad_attn.astype(jnp.float32)
    own_s = jnp.einsum('phe,khe->hpk', query_f, keys_own.astype(jnp.float32)) * scale
    prev_s = jnp.einsum('phe,khe->hpk', query_f, keys_prev.astype(jnp.float32)) * scale
    row_top = jnp.maximum(lax.optimization_barrier(jnp.max(own_s, axis=-1)), jnp.where(has_prev > 0.5, lax.optimization_barrier(jnp.max(prev_s, axis=-1)), -1e+30))
    own_e = jnp.exp(own_s - row_top[..., None])
    prev_e = jnp.exp(prev_s - row_top[..., None]) * has_prev
    row_total = lax.optimization_barrier(jnp.sum(own_e, axis=-1)) + lax.optimization_barrier(jnp.sum(prev_e, axis=-1))
    own_p = own_e / row_total[..., None]
    prev_p = prev_e / row_total[..., None]
    own_dp = jnp.einsum('phe,khe->hpk', grad_f, values_own.astype(jnp.float32))
    prev_dp = jnp.einsum('phe,khe->hpk', grad_f, values_prev.astype(jnp.float32))
    row_delta = lax.optimization_barrier(jnp.sum(own_p * own_dp, axis=-1)) + lax.optimization_barrier(jnp.sum(prev_p * prev_dp, axis=-1))
    own_ds = round_keep(own_p * (own_dp - row_delta[..., None]) * scale)
    prev_ds = round_keep(prev_p * (prev_dp - row_delta[..., None]) * scale)
    own_pb = round_keep(own_p)
    prev_pb = round_keep(prev_p)
    grad_query = (jnp.einsum('hpk,khe->phe', own_ds, keys_own.astype(jnp.float32)) + jnp.einsum('hpk,khe->phe', prev_ds, keys_prev.astype(jnp.float32))).astype(jnp.bfloat16)
    key_own_g = jnp.einsum('hpk,phe->khe', own_ds, query_f)
    value_own_g = jnp.einsum('hpk,phe->khe', own_pb, grad_f)
    key_back_g = jnp.einsum('hpk,phe->khe', prev_ds, query_f)
    value_back_g = jnp.einsum('hpk,phe->khe', prev_pb, grad_f)
    return (grad_query, key_own_g, value_own_g, key_back_g, value_back_g)

def reference(latents, cotangent, norm_gain, w_qkv, w_out):
    frames = N_TM
    latent_f = latents.astype(jnp.float32)
    inv_rms = lax.rsqrt(lax.optimization_barrier(jnp.mean(latent_f * latent_f, axis=-1, keepdims=True)) + EPSILON)
    normed = latent_f * inv_rms
    hidden = (normed * norm_gain).astype(jnp.bfloat16)
    flat_w = w_qkv.reshape(D, 3 * D)
    projected = jnp.dot(hidden, flat_w, preferred_element_type=jnp.float32).astype(jnp.bfloat16)
    shape4 = (frames, FRAME_TOK, HEADS, HEAD_DIM)
    queries = projected[:, :D].reshape(shape4)
    keys_all = projected[:, D:2 * D].reshape(shape4)
    values_all = projected[:, 2 * D:].reshape(shape4)
    grad_attn = jnp.dot(cotangent, w_out.T, preferred_element_type=jnp.float32).astype(jnp.bfloat16).reshape(shape4)
    keys_prev = jnp.concatenate([jnp.zeros_like(keys_all[:1]), keys_all[:-1]], axis=0)
    values_prev = jnp.concatenate([jnp.zeros_like(values_all[:1]), values_all[:-1]], axis=0)
    has_prev = (jnp.arange(frames) > 0).astype(jnp.float32)
    grad_query, key_own_g, value_own_g, key_back_g, value_back_g = lax.map(frame_grads, (queries, keys_all, keys_prev, values_all, values_prev, grad_attn, has_prev))
    key_next = jnp.concatenate([key_back_g[1:], jnp.zeros_like(key_back_g[:1])], axis=0)
    value_next = jnp.concatenate([value_back_g[1:], jnp.zeros_like(value_back_g[:1])], axis=0)
    grad_key = (key_own_g + round_keep(key_next)).astype(jnp.bfloat16)
    grad_value = (value_own_g + round_keep(value_next)).astype(jnp.bfloat16)
    grad_qkv = jnp.stack([grad_query.reshape(TOKENS, D), grad_key.reshape(TOKENS, D), grad_value.reshape(TOKENS, D)], axis=1)
    group_width = D // N_HEAD
    grad_hidden = jnp.zeros((TOKENS, D), jnp.float32)
    for group_index in range(N_HEAD):
        first_col = group_index * group_width
        grad_part = grad_qkv[:, :, first_col:first_col + group_width].reshape(TOKENS, 3 * group_width)
        weight_part = w_qkv[:, :, first_col:first_col + group_width].reshape(D, 3 * group_width)
        partial_sum = lax.dot_general(grad_part, weight_part, (((1,), (1,)), ((), ())), preferred_element_type=jnp.float32)
        grad_hidden = grad_hidden + round_keep(partial_sum)
    grad_normed = grad_hidden * norm_gain
    inner = lax.optimization_barrier(jnp.mean(grad_normed * normed, axis=-1, keepdims=True))
    result = cotangent.astype(jnp.float32) + inv_rms * (grad_normed - normed * inner)
    return result.astype(jnp.bfloat16)
```

```python
import functools

import jax
import jax.numpy as jnp
from jax import lax
from jax.experimental import pallas as pl
from jax.experimental.pallas import tpu as pltpu
from jax.sharding import PartitionSpec as P

EPSILON = 1e-06
MESH = pl.DeviceIdType.MESH
D = 3072
HEAD_DIM = 128
HEADS_HERE = 3
WIDTH = HEADS_HERE * HEAD_DIM
BLOCK = 64
HALF = BLOCK // 2
FRAME = 512
PAIR = 2 * BLOCK
COLS = D // 2
N_TM = 32
X = 4
SCALE = HEAD_DIM ** (-0.5)
BF = jnp.bfloat16
F32 = jnp.float32


def nt(a, b):
    return lax.dot_general(a, b, (((1,), (1,)), ((), ())), preferred_element_type=F32)


def nn(a, b):
    return jnp.dot(a, b, preferred_element_type=F32)


def kernel(
    lat_h, cot_h, gain_h, wqkv_h, wout_h, out_ref,
    lat, gain, wq, wo, hid, cot, inv, q, kv, kt, probs, acc_k, acc_v, back_s, back_r, g,
    part, ra, rb, rl, rr, zs, rz, ga_s, grad,
    ld_sem, gs_sem, gr_sem, kvs_sem, kvr_sem, bs_sem, br_sem, rs_sem, rr_sem, zs_sem, zr_sem,
):
    tm = lax.axis_index("tm")
    head = lax.axis_index("head")
    x = lax.rem(head, X)
    base = head - x
    right = (tm, base + lax.rem(x + 1, X))
    left = (tm, base + lax.rem(x + X - 1, X))
    across = (tm, lax.rem(head + X, 2 * X))
    after = (lax.rem(tm + 1, N_TM), head)
    before = (lax.rem(tm + N_TM - 1, N_TM), head)

    barrier = pltpu.get_barrier_semaphore()
    for peer in (right, left, across, after, before):
        pl.semaphore_signal(barrier, inc=1, device_id=peer, device_id_type=MESH)

    loads = [
        pltpu.make_async_copy(lat_h, lat, ld_sem.at[0]),
        pltpu.make_async_copy(gain_h, gain, ld_sem.at[1]),
        pltpu.make_async_copy(cot_h, cot.at[pl.ds(0, BLOCK)], ld_sem.at[2]),
        pltpu.make_async_copy(wqkv_h, wq, ld_sem.at[3]),
        pltpu.make_async_copy(wout_h, wo, ld_sem.at[4]),
    ]
    for load in loads:
        load.start()
    loads[0].wait()
    loads[1].wait()
    for r in range(4):
        rows = pl.ds(r * 16, 16)
        lf = lat[rows].astype(F32)
        scale = lax.rsqrt(jnp.mean(lf * lf, axis=-1, keepdims=True) + EPSILON)
        inv[rows] = jnp.broadcast_to(scale, (16, 128))
        hid[rows] = (lf * scale * gain[...]).astype(BF)
    pl.semaphore_wait(barrier, 5)

    sent = []

    def push(src, dst, s_sem, r_sem, peer):
        copy = pltpu.make_async_remote_copy(
            src_ref=src, dst_ref=dst, send_sem=s_sem, recv_sem=r_sem, device_id=peer, device_id_type=MESH
        )
        copy.start()
        sent.append(copy)
        return copy

    def chunk(slot, c):
        return pl.ds(slot * BLOCK + c * HALF, HALF)

    bufs = (hid, cot)
    moves = {}

    def gather_push(a, src_slot, dst_slot, c, peer):
        i = dst_slot * 2 + c
        moves[a, dst_slot, c] = push(
            bufs[a].at[chunk(src_slot, c)], bufs[a].at[chunk(dst_slot, c)], gs_sem.at[a, i], gr_sem.at[a, i], peer
        )

    def got(a, slot, c):
        moves[a, slot, c].wait_recv()

    def spread(a, zz, cs):
        for c in cs:
            gather_push(a, 4 * zz, 4 * zz + 1, c, right)
            gather_push(a, 4 * zz, 4 * zz + 2, 1 - c if len(cs) == 2 else c, left)

    def forward(a, zz):
        got(a, 4 * zz + 1, 0)
        gather_push(a, 4 * zz + 1, 4 * zz + 3, 0, right)
        got(a, 4 * zz + 2, 1)
        gather_push(a, 4 * zz + 2, 4 * zz + 3, 1, left)

    kv_copies = []

    def project(p):
        rows = pl.ds(p * PAIR, PAIR)
        h = hid[rows]
        q[rows] = nn(h, wq[0]).astype(BF)
        kv[rows, pl.ds(0, WIDTH)] = nn(h, wq[1]).astype(BF)
        kv[rows, pl.ds(WIDTH, WIDTH)] = nn(h, wq[2]).astype(BF)
        kv_copies.append(
            push(kv.at[rows], kv.at[pl.ds(FRAME + p * PAIR, PAIR)], kvs_sem.at[p], kvr_sem.at[p], after)
        )

    for c in (0, 1):
        gather_push(0, 0, 4, c, across)
    spread(0, 0, (0, 1))
    loads[2].wait()
    forward(0, 0)
    spread(1, 0, (0, 1))
    loads[3].wait()
    got(0, 1, 1)
    project(0)
    got(0, 4, 0)
    spread(0, 1, (0,))
    got(0, 2, 0)
    got(0, 3, 0)
    got(0, 3, 1)
    project(1)
    got(0, 4, 1)
    spread(0, 1, (1,))
    for c in (0, 1):
        gather_push(1, 0, 4, c, across)
    forward(1, 0)
    forward(0, 1)
    got(0, 5, 1)
    project(2)
    got(1, 4, 0)
    spread(1, 1, (0,))
    got(0, 6, 0)
    got(0, 7, 0)
    got(0, 7, 1)
    project(3)
    got(1, 4, 1)
    spread(1, 1, (1,))
    loads[4].wait()

    def lanes(h):
        return pl.ds(pl.multiple_of(h * HEAD_DIM, HEAD_DIM), HEAD_DIM)

    def v_lanes(h):
        return pl.ds(pl.multiple_of(WIDTH + h * HEAD_DIM, HEAD_DIM), HEAD_DIM)

    acc_k[...] = jnp.zeros_like(acc_k)
    acc_v[...] = jnp.zeros_like(acc_v)
    for copy in kv_copies:
        copy.wait_recv()

    def turn(h, carry):
        kt[h] = kv[:, lanes(h)].astype(F32).T.astype(BF)
        return carry

    lax.fori_loop(0, HEADS_HERE, turn, 0)

    def score(i, carry):
        p = i // HEADS_HERE
        h = i - p * HEADS_HERE
        rows = pl.ds(pl.multiple_of(p * PAIR, PAIR), PAIR)
        qh = q[rows, lanes(h)]
        own = nt(kv[pl.ds(0, FRAME), lanes(h)], qh) * SCALE
        prev = nt(kv[pl.ds(FRAME, FRAME), lanes(h)], qh) * SCALE
        prev = jnp.where(tm > 0, prev, -1e30)
        top = jnp.maximum(jnp.max(own, axis=0, keepdims=True), jnp.max(prev, axis=0, keepdims=True))
        own = jnp.exp(own - top)
        prev = jnp.exp(prev - top)
        total = jnp.sum(own, axis=0, keepdims=True) + jnp.sum(prev, axis=0, keepdims=True)
        part_of = 1.0 / total
        probs[i, pl.ds(0, FRAME)] = own * part_of
        probs[i, pl.ds(FRAME, FRAME)] = prev * part_of
        return carry

    lax.fori_loop(0, 2 * HEADS_HERE, score, 0)
    forward(1, 1)
    lax.fori_loop(2 * HEADS_HERE, 4 * HEADS_HERE, score, 0)

    def backward(p):
        rows = pl.ds(p * PAIR, PAIR)
        ga_all = nt(cot[rows], wo[...]).astype(BF)
        ga_s[...] = ga_all

        def one(h, carry):
            ga = ga_s[:, lanes(h)]
            pt = probs[p * HEADS_HERE + h]
            dp = nt(kv[:, v_lanes(h)], ga)
            delta = jnp.sum(pt * dp, axis=0, keepdims=True)
            ds = (pt * (dp - delta) * SCALE).astype(BF)
            acc_k[:, lanes(h)] += nn(ds, q[rows, lanes(h)])
            acc_v[:, lanes(h)] += nn(pt.astype(BF), ga)
            g[rows, lanes(h)] = nn(kt[h], ds).T.astype(BF)
            return carry

        lax.fori_loop(0, HEADS_HERE, one, 0)

    got(1, 1, 1)
    backward(0)
    got(1, 2, 0)
    got(1, 3, 0)
    got(1, 3, 1)
    backward(1)
    got(1, 5, 1)
    backward(2)
    got(1, 6, 0)
    got(1, 7, 0)
    got(1, 7, 1)
    backward(3)

    backs = {}
    for zz in (1, 0):
        rows = pl.ds(zz * 256, 256)
        theirs = pl.ds(FRAME + zz * 256, 256)
        back_s[rows, pl.ds(0, WIDTH)] = acc_k[theirs].astype(BF)
        back_s[rows, pl.ds(WIDTH, WIDTH)] = acc_v[theirs].astype(BF)
        backs[zz] = push(back_s.at[rows], back_r.at[rows], bs_sem.at[zz], br_sem.at[zz], before)

    def join(zz):
        rows = pl.ds(zz * 256, 256)
        backs[zz].wait_recv()
        g[rows, pl.ds(WIDTH, WIDTH)] = (acc_k[rows] + back_r[rows, pl.ds(0, WIDTH)].astype(F32)).astype(BF)
        g[rows, pl.ds(2 * WIDTH, WIDTH)] = (acc_v[rows] + back_r[rows, pl.ds(WIDTH, WIDTH)].astype(F32)).astype(BF)

    def partials(zz, hf):
        def tile(n, carry):
            w_rows = pl.ds(pl.multiple_of(hf * COLS + n * 512, 512), 512)
            rows = pl.ds(zz * 256, 256)
            total = nt(g[rows, pl.ds(0, WIDTH)], wq[0, w_rows])
            total += nt(g[rows, pl.ds(WIDTH, WIDTH)], wq[1, w_rows])
            total += nt(g[rows, pl.ds(2 * WIDTH, WIDTH)], wq[2, w_rows])
            part[hf, rows, pl.ds(pl.multiple_of(n * 512, 512), 512)] = total.astype(BF)
            return carry

        lax.fori_loop(0, COLS // 512, tile, 0)

    sums = {}

    def sum_push(key, i, src, dst, peer):
        zz, hf = key
        k = (zz * 2 + hf) * 6 + i
        sums[key, i] = push(src, dst, rs_sem.at[k], rr_sem.at[k], peer)

    def opposite(zz, hf):
        u = zz * 2 + hf
        sum_push((zz, hf), 0, part.at[hf, chunk(4 * zz + 3, 0)], ra.at[u], right)
        sum_push((zz, hf), 1, part.at[hf, chunk(4 * zz + 3, 1)], rb.at[u], left)

    def singles(zz, hf):
        u = zz * 2 + hf
        sum_push((zz, hf), 2, part.at[hf, chunk(4 * zz + 2, 1)], rl.at[u, pl.ds(HALF, HALF)], right)
        sum_push((zz, hf), 3, part.at[hf, chunk(4 * zz + 1, 0)], rr.at[u, pl.ds(0, HALF)], left)

    def doubles(zz, hf):
        u = zz * 2 + hf
        to_right = chunk(4 * zz + 2, 0)
        to_left = chunk(4 * zz + 1, 1)
        sums[(zz, hf), 0].wait_recv()
        part[hf, to_right] = (part[hf, to_right].astype(F32) + ra[u].astype(F32)).astype(BF)
        sum_push((zz, hf), 4, part.at[hf, to_right], rl.at[u, pl.ds(0, HALF)], right)
        sums[(zz, hf), 1].wait_recv()
        part[hf, to_left] = (part[hf, to_left].astype(F32) + rb[u].astype(F32)).astype(BF)
        sum_push((zz, hf), 5, part.at[hf, to_left], rr.at[u, pl.ds(HALF, HALF)], left)

    crossing = {}

    def cross(hf):
        for i in (2, 3, 4, 5):
            sums[(1, hf), i].wait_recv()
        mine = part[hf, pl.ds(256, BLOCK)].astype(F32)
        zs[hf] = (mine + rl[2 + hf].astype(F32) + rr[2 + hf].astype(F32)).astype(BF)
        crossing[hf] = push(zs.at[hf], rz.at[hf], zs_sem.at[hf], zr_sem.at[hf], across)

    join(1)
    partials(1, 0)
    opposite(1, 0)
    singles(1, 0)
    partials(1, 1)
    opposite(1, 1)
    doubles(1, 0)
    singles(1, 1)
    join(0)
    partials(0, 0)
    opposite(0, 0)
    doubles(1, 1)
    cross(0)
    singles(0, 0)
    partials(0, 1)
    opposite(0, 1)
    doubles(0, 0)
    cross(1)
    singles(0, 1)
    doubles(0, 1)
    for hf in (0, 1):
        for i in (2, 3, 4, 5):
            sums[(0, hf), i].wait_recv()
    for hf in (0, 1):
        crossing[hf].wait_recv()

    for r in range(4):
        rows = pl.ds(r * 16, 16)
        scale = inv[rows, pl.ds(0, 1)]
        inner = jnp.zeros((16, 1), F32)
        for hf in (0, 1):
            cols = pl.ds(hf * COLS, COLS)
            total = (
                part[hf, rows].astype(F32) + rl[hf, rows].astype(F32) + rr[hf, rows].astype(F32)
                + rz[hf, rows].astype(F32)
            )
            total = total * gain[:, cols]
            inner += jnp.sum(total * (lat[rows, cols].astype(F32) * scale), axis=-1, keepdims=True)
            grad[rows, cols] = total
        inner = inner * (1.0 / D)
        normed = lat[rows].astype(F32) * scale
        out_ref[rows] = (cot[rows].astype(F32) + scale * (grad[rows] - normed * inner)).astype(BF)

    for copy in sent:
        copy.wait_send()


def shards(latents, cotangent, norm_gain, w_qkv, w_out):
    hbm = pl.BlockSpec(memory_space=pl.ANY)
    dma = pltpu.SemaphoreType.DMA
    return pl.pallas_call(
        kernel,
        out_shape=jax.ShapeDtypeStruct((BLOCK, D), BF),
        in_specs=[hbm] * 5,
        out_specs=pl.BlockSpec(memory_space=pltpu.VMEM),
        scratch_shapes=[
            pltpu.VMEM((BLOCK, D), BF),
            pltpu.VMEM((1, D), F32),
            pltpu.VMEM((3, D, WIDTH), BF),
            pltpu.VMEM((WIDTH, D), BF),
            pltpu.VMEM((FRAME, D), BF),
            pltpu.VMEM((FRAME, D), BF),
            pltpu.VMEM((BLOCK, 128), F32),
            pltpu.VMEM((FRAME, WIDTH), BF),
            pltpu.VMEM((2 * FRAME, 2 * WIDTH), BF),
            pltpu.VMEM((HEADS_HERE, HEAD_DIM, 2 * FRAME), BF),
            pltpu.VMEM((4 * HEADS_HERE, 2 * FRAME, PAIR), F32),
            pltpu.VMEM((2 * FRAME, WIDTH), F32),
            pltpu.VMEM((2 * FRAME, WIDTH), F32),
            pltpu.VMEM((FRAME, 2 * WIDTH), BF),
            pltpu.VMEM((FRAME, 2 * WIDTH), BF),
            pltpu.VMEM((FRAME, 3 * WIDTH), BF),
            pltpu.VMEM((2, FRAME, COLS), BF),
            pltpu.VMEM((4, HALF, COLS), BF),
            pltpu.VMEM((4, HALF, COLS), BF),
            pltpu.VMEM((4, BLOCK, COLS), BF),
            pltpu.VMEM((4, BLOCK, COLS), BF),
            pltpu.VMEM((2, BLOCK, COLS), BF),
            pltpu.VMEM((2, BLOCK, COLS), BF),
            pltpu.VMEM((PAIR, WIDTH), BF),
            pltpu.VMEM((BLOCK, D), F32),
            dma((5,)),
            dma((2, 16)),
            dma((2, 16)),
            dma((4,)),
            dma((4,)),
            dma((2,)),
            dma((2,)),
            dma((24,)),
            dma((24,)),
            dma((2,)),
            dma((2,)),
        ],
        compiler_params=pltpu.CompilerParams(
            collective_id=0, has_side_effects=True, vmem_limit_bytes=56 * 1024 * 1024
        ),
        name="frame_attention_grad",
    )(latents, cotangent, norm_gain.reshape(1, D), jnp.transpose(w_qkv, (1, 0, 2)), w_out)


def solution(mesh):
    return jax.shard_map(
        shards,
        mesh=mesh,
        in_specs=(
            P(("tm", "head"), None),
            P(("tm", "head"), None),
            P(),
            P(None, None, "head"),
            P("head", None),
        ),
        out_specs=P(("tm", "head"), None),
        check_vma=False,
    )
```

```python
import functools

import jax
import jax.numpy as jnp
from jax import lax
from jax.experimental import pallas as pl
from jax.experimental.pallas import tpu as pltpu
from jax.sharding import PartitionSpec as P

EPSILON = 1e-06
MESH = pl.DeviceIdType.MESH
D = 3072
HEAD_DIM = 128
HEADS_HERE = 3
WIDTH = HEADS_HERE * HEAD_DIM
BLOCK = 64
HALF = BLOCK // 2
FRAME = 512
PAIR = 2 * BLOCK
COLS = D // 2
N_TM = 32
X = 4
SCALE = HEAD_DIM ** (-0.5)
BF = jnp.bfloat16
F32 = jnp.float32


def nt(a, b):
    return lax.dot_general(a, b, (((1,), (1,)), ((), ())), preferred_element_type=F32)


def nn(a, b):
    return jnp.dot(a, b, preferred_element_type=F32)


def kernel(
    lat_h, cot_h, gain_h, wqkv_h, wout_h, out_ref,
    lat, gain, wq, wo, hid, cot, inv, q, kv, kt, probs, acc_k, acc_v, back_s, back_r, g,
    part, ra, rb, rl, rr, zs, rz, ga_s, ds_s, grad,
    ld_sem, gs_sem, gr_sem, kvs_sem, kvr_sem, bs_sem, br_sem, rs_sem, rr_sem, zs_sem, zr_sem,
):
    tm = lax.axis_index("tm")
    head = lax.axis_index("head")
    x = lax.rem(head, X)
    base = head - x
    right = (tm, base + lax.rem(x + 1, X))
    left = (tm, base + lax.rem(x + X - 1, X))
    across = (tm, lax.rem(head + X, 2 * X))
    after = (lax.rem(tm + 1, N_TM), head)
    before = (lax.rem(tm + N_TM - 1, N_TM), head)

    barrier = pltpu.get_barrier_semaphore()
    for peer in (right, left, across, after, before):
        pl.semaphore_signal(barrier, inc=1, device_id=peer, device_id_type=MESH)

    loads = [
        pltpu.make_async_copy(lat_h, lat, ld_sem.at[0]),
        pltpu.make_async_copy(gain_h, gain, ld_sem.at[1]),
        pltpu.make_async_copy(cot_h, cot.at[pl.ds(0, BLOCK)], ld_sem.at[2]),
        pltpu.make_async_copy(wqkv_h, wq, ld_sem.at[3]),
        pltpu.make_async_copy(wout_h, wo, ld_sem.at[4]),
    ]
    for load in loads:
        load.start()
    loads[0].wait()
    loads[1].wait()
    for r in range(4):
        rows = pl.ds(r * 16, 16)
        lf = lat[rows].astype(F32)
        scale = lax.rsqrt(jnp.mean(lf * lf, axis=-1, keepdims=True) + EPSILON)
        inv[rows] = jnp.broadcast_to(scale, (16, 128))
        hid[rows] = (lf * scale * gain[...]).astype(BF)
    pl.semaphore_wait(barrier, 5)

    sent = []

    def push(src, dst, s_sem, r_sem, peer):
        copy = pltpu.make_async_remote_copy(
            src_ref=src, dst_ref=dst, send_sem=s_sem, recv_sem=r_sem, device_id=peer, device_id_type=MESH
        )
        copy.start()
        sent.append(copy)
        return copy

    def chunk(slot, c):
        return pl.ds(slot * BLOCK + c * HALF, HALF)

    bufs = (hid, cot)
    moves = {}

    def gather_push(a, src_slot, dst_slot, c, peer):
        i = dst_slot * 2 + c
        moves[a, dst_slot, c] = push(
            bufs[a].at[chunk(src_slot, c)], bufs[a].at[chunk(dst_slot, c)], gs_sem.at[a, i], gr_sem.at[a, i], peer
        )

    def got(a, slot, c):
        moves[a, slot, c].wait_recv()

    def spread(a, zz, cs):
        for c in cs:
            gather_push(a, 4 * zz, 4 * zz + 1, c, right)
            gather_push(a, 4 * zz, 4 * zz + 2, 1 - c if len(cs) == 2 else c, left)

    def forward_right(a, zz):
        got(a, 4 * zz + 1, 0)
        gather_push(a, 4 * zz + 1, 4 * zz + 3, 0, right)

    def forward_left(a, zz):
        got(a, 4 * zz + 2, 1)
        gather_push(a, 4 * zz + 2, 4 * zz + 3, 1, left)

    def forward(a, zz):
        forward_right(a, zz)
        forward_left(a, zz)

    kv_copies = []

    def project(p):
        rows = pl.ds(p * PAIR, PAIR)
        h = hid[rows]
        q[rows] = nn(h, wq[0]).astype(BF)
        kv[rows, pl.ds(0, WIDTH)] = nn(h, wq[1]).astype(BF)
        kv[rows, pl.ds(WIDTH, WIDTH)] = nn(h, wq[2]).astype(BF)
        kv_copies.append(
            push(kv.at[rows], kv.at[pl.ds(FRAME + p * PAIR, PAIR)], kvs_sem.at[p], kvr_sem.at[p], after)
        )

    for c in (0, 1):
        gather_push(0, 0, 4, c, across)
    spread(0, 0, (0, 1))
    loads[2].wait()
    forward(0, 0)
    gather_push(1, 0, 1, 0, right)
    gather_push(1, 0, 2, 1, left)
    loads[3].wait()
    got(0, 1, 1)
    project(0)
    got(0, 4, 0)
    spread(0, 1, (0,))
    got(0, 2, 0)
    got(0, 3, 0)
    got(0, 3, 1)
    project(1)
    got(0, 4, 1)
    spread(0, 1, (1,))
    for c in (0, 1):
        gather_push(1, 0, 4, c, across)
    forward(0, 1)
    gather_push(1, 0, 1, 1, right)
    gather_push(1, 0, 2, 0, left)
    got(0, 5, 1)
    project(2)
    forward(1, 0)
    got(1, 4, 0)
    spread(1, 1, (0,))
    got(0, 6, 0)
    got(0, 7, 0)
    got(0, 7, 1)
    project(3)
    loads[4].wait()

    def lanes(h):
        return pl.ds(pl.multiple_of(h * HEAD_DIM, HEAD_DIM), HEAD_DIM)

    def v_lanes(h):
        return pl.ds(pl.multiple_of(WIDTH + h * HEAD_DIM, HEAD_DIM), HEAD_DIM)

    acc_k[...] = jnp.zeros_like(acc_k)
    acc_v[...] = jnp.zeros_like(acc_v)
    for copy in kv_copies:
        copy.wait_recv()

    def turn(h, carry):
        kt[h] = kv[:, lanes(h)].astype(F32).T.astype(BF)
        return carry

    lax.fori_loop(0, HEADS_HERE, turn, 0)

    def score(i, carry):
        p = i // HEADS_HERE
        h = i - p * HEADS_HERE
        rows = pl.ds(pl.multiple_of(p * PAIR, PAIR), PAIR)
        qh = q[rows, lanes(h)]
        own = nt(kv[pl.ds(0, FRAME), lanes(h)], qh) * SCALE
        prev = nt(kv[pl.ds(FRAME, FRAME), lanes(h)], qh) * SCALE
        prev = jnp.where(tm > 0, prev, -1e30)
        top = jnp.maximum(jnp.max(own, axis=0, keepdims=True), jnp.max(prev, axis=0, keepdims=True))
        own = jnp.exp(own - top)
        prev = jnp.exp(prev - top)
        total = jnp.sum(own, axis=0, keepdims=True) + jnp.sum(prev, axis=0, keepdims=True)
        part_of = 1.0 / total
        probs[i, pl.ds(0, FRAME)] = own * part_of
        probs[i, pl.ds(FRAME, FRAME)] = prev * part_of
        return carry

    lax.fori_loop(0, 2 * HEADS_HERE, score, 0)
    got(1, 4, 1)
    spread(1, 1, (1,))
    lax.fori_loop(2 * HEADS_HERE, 4 * HEADS_HERE, score, 0)

    def score_grads(p, h):
        pt = probs[p * HEADS_HERE + h]
        dp = nt(kv[:, v_lanes(h)], ga_s[:, lanes(h)])
        delta = jnp.sum(pt * dp, axis=0, keepdims=True)
        return pt, (pt * (dp - delta) * SCALE).astype(BF)

    def backward(p):
        rows = pl.ds(p * PAIR, PAIR)
        ga_s[...] = nt(cot[rows], wo[...]).astype(BF)

        def one(h, carry):
            pt, ds = score_grads(p, h)
            acc_k[:, lanes(h)] += nn(ds, q[rows, lanes(h)])
            acc_v[:, lanes(h)] += nn(pt.astype(BF), ga_s[:, lanes(h)])
            g[rows, lanes(h)] = nn(kt[h], ds).T.astype(BF)
            return carry

        lax.fori_loop(0, HEADS_HERE, one, 0)

    forward_right(1, 1)
    got(1, 1, 1)
    backward(0)
    forward_left(1, 1)
    got(1, 2, 0)
    got(1, 3, 0)
    got(1, 3, 1)
    backward(1)
    got(1, 5, 1)
    backward(2)
    got(1, 6, 0)
    got(1, 7, 0)
    got(1, 7, 1)

    last = pl.ds(3 * PAIR, PAIR)
    own = pl.ds(0, FRAME)
    prev = pl.ds(FRAME, FRAME)
    ga_s[...] = nt(cot[last], wo[...]).astype(BF)

    def last_prev(h, carry):
        pt, ds = score_grads(3, h)
        ds_s[h] = ds
        back_s[:, lanes(h)] = (acc_k[prev, lanes(h)] + nn(ds[FRAME:], q[last, lanes(h)])).astype(BF)
        back_s[:, v_lanes(h)] = (acc_v[prev, lanes(h)] + nn(pt[FRAME:].astype(BF), ga_s[:, lanes(h)])).astype(BF)
        return carry

    lax.fori_loop(0, HEADS_HERE, last_prev, 0)
    pieces = ((448, 64), (256, 192), (0, 256))
    backs = []
    for i, (start, size) in enumerate(pieces):
        rows = pl.ds(start, size)
        backs.append(push(back_s.at[rows], back_r.at[rows], bs_sem.at[i], br_sem.at[i], before))

    def last_own(h, carry):
        g[last, lanes(h)] = nn(kt[h], ds_s[h]).T.astype(BF)
        acc_k[own, lanes(h)] += nn(ds_s[h, own], q[last, lanes(h)])
        acc_v[own, lanes(h)] += nn(probs[3 * HEADS_HERE + h, own].astype(BF), ga_s[:, lanes(h)])
        return carry

    lax.fori_loop(0, HEADS_HERE, last_own, 0)

    def join(i):
        rows = pl.ds(*pieces[i])
        backs[i].wait_recv()
        g[rows, pl.ds(WIDTH, WIDTH)] = (acc_k[rows] + back_r[rows, pl.ds(0, WIDTH)].astype(F32)).astype(BF)
        g[rows, pl.ds(2 * WIDTH, WIDTH)] = (acc_v[rows] + back_r[rows, pl.ds(WIDTH, WIDTH)].astype(F32)).astype(BF)

    def partials(i, hf):
        rows = pl.ds(*pieces[i])

        def tile(n, carry):
            w_rows = pl.ds(pl.multiple_of(hf * COLS + n * 512, 512), 512)
            total = nt(g[rows, pl.ds(0, WIDTH)], wq[0, w_rows])
            total += nt(g[rows, pl.ds(WIDTH, WIDTH)], wq[1, w_rows])
            total += nt(g[rows, pl.ds(2 * WIDTH, WIDTH)], wq[2, w_rows])
            part[hf, rows, pl.ds(pl.multiple_of(n * 512, 512), 512)] = total.astype(BF)
            return carry

        lax.fori_loop(0, COLS // 512, tile, 0)

    sums = {}

    def sum_push(key, i, src, dst, peer):
        zz, hf = key
        k = (zz * 2 + hf) * 6 + i
        sums[key, i] = push(src, dst, rs_sem.at[k], rr_sem.at[k], peer)

    def opposite(zz, hf):
        u = zz * 2 + hf
        sum_push((zz, hf), 0, part.at[hf, chunk(4 * zz + 3, 0)], ra.at[u], right)
        sum_push((zz, hf), 1, part.at[hf, chunk(4 * zz + 3, 1)], rb.at[u], left)

    def singles(zz, hf):
        u = zz * 2 + hf
        sum_push((zz, hf), 2, part.at[hf, chunk(4 * zz + 2, 1)], rl.at[u, pl.ds(HALF, HALF)], right)
        sum_push((zz, hf), 3, part.at[hf, chunk(4 * zz + 1, 0)], rr.at[u, pl.ds(0, HALF)], left)

    def doubles(zz, hf):
        u = zz * 2 + hf
        to_right = chunk(4 * zz + 2, 0)
        to_left = chunk(4 * zz + 1, 1)
        sums[(zz, hf), 0].wait_recv()
        part[hf, to_right] = (part[hf, to_right].astype(F32) + ra[u].astype(F32)).astype(BF)
        sum_push((zz, hf), 4, part.at[hf, to_right], rl.at[u, pl.ds(0, HALF)], right)
        sums[(zz, hf), 1].wait_recv()
        part[hf, to_left] = (part[hf, to_left].astype(F32) + rb[u].astype(F32)).astype(BF)
        sum_push((zz, hf), 5, part.at[hf, to_left], rr.at[u, pl.ds(HALF, HALF)], left)

    crossing = {}

    def cross(hf):
        for i in (2, 3, 4, 5):
            sums[(1, hf), i].wait_recv()
        mine = part[hf, pl.ds(256, BLOCK)].astype(F32)
        zs[hf] = (mine + rl[2 + hf].astype(F32) + rr[2 + hf].astype(F32)).astype(BF)
        crossing[hf] = push(zs.at[hf], rz.at[hf], zs_sem.at[hf], zr_sem.at[hf], across)

    join(0)
    partials(0, 0)
    opposite(1, 0)
    partials(0, 1)
    opposite(1, 1)
    join(1)
    partials(1, 0)
    singles(1, 0)
    doubles(1, 0)
    partials(1, 1)
    singles(1, 1)
    doubles(1, 1)
    join(2)
    partials(2, 0)
    opposite(0, 0)
    singles(0, 0)
    cross(0)
    partials(2, 1)
    opposite(0, 1)
    doubles(0, 0)
    cross(1)
    singles(0, 1)
    doubles(0, 1)
    for hf in (0, 1):
        for i in (2, 3, 4, 5):
            sums[(0, hf), i].wait_recv()
    for hf in (0, 1):
        crossing[hf].wait_recv()

    for r in range(4):
        rows = pl.ds(r * 16, 16)
        scale = inv[rows, pl.ds(0, 1)]
        inner = jnp.zeros((16, 1), F32)
        for hf in (0, 1):
            cols = pl.ds(hf * COLS, COLS)
            total = (
                part[hf, rows].astype(F32) + rl[hf, rows].astype(F32) + rr[hf, rows].astype(F32)
                + rz[hf, rows].astype(F32)
            )
            total = total * gain[:, cols]
            inner += jnp.sum(total * (lat[rows, cols].astype(F32) * scale), axis=-1, keepdims=True)
            grad[rows, cols] = total
        inner = inner * (1.0 / D)
        normed = lat[rows].astype(F32) * scale
        out_ref[rows] = (cot[rows].astype(F32) + scale * (grad[rows] - normed * inner)).astype(BF)

    for copy in sent:
        copy.wait_send()


def shards(latents, cotangent, norm_gain, w_qkv, w_out):
    hbm = pl.BlockSpec(memory_space=pl.ANY)
    dma = pltpu.SemaphoreType.DMA
    return pl.pallas_call(
        kernel,
        out_shape=jax.ShapeDtypeStruct((BLOCK, D), BF),
        in_specs=[hbm] * 5,
        out_specs=pl.BlockSpec(memory_space=pltpu.VMEM),
        scratch_shapes=[
            pltpu.VMEM((BLOCK, D), BF),
            pltpu.VMEM((1, D), F32),
            pltpu.VMEM((3, D, WIDTH), BF),
            pltpu.VMEM((WIDTH, D), BF),
            pltpu.VMEM((FRAME, D), BF),
            pltpu.VMEM((FRAME, D), BF),
            pltpu.VMEM((BLOCK, 128), F32),
            pltpu.VMEM((FRAME, WIDTH), BF),
            pltpu.VMEM((2 * FRAME, 2 * WIDTH), BF),
            pltpu.VMEM((HEADS_HERE, HEAD_DIM, 2 * FRAME), BF),
            pltpu.VMEM((4 * HEADS_HERE, 2 * FRAME, PAIR), F32),
            pltpu.VMEM((2 * FRAME, WIDTH), F32),
            pltpu.VMEM((2 * FRAME, WIDTH), F32),
            pltpu.VMEM((FRAME, 2 * WIDTH), BF),
            pltpu.VMEM((FRAME, 2 * WIDTH), BF),
            pltpu.VMEM((FRAME, 3 * WIDTH), BF),
            pltpu.VMEM((2, FRAME, COLS), BF),
            pltpu.VMEM((4, HALF, COLS), BF),
            pltpu.VMEM((4, HALF, COLS), BF),
            pltpu.VMEM((4, BLOCK, COLS), BF),
            pltpu.VMEM((4, BLOCK, COLS), BF),
            pltpu.VMEM((2, BLOCK, COLS), BF),
            pltpu.VMEM((2, BLOCK, COLS), BF),
            pltpu.VMEM((PAIR, WIDTH), BF),
            pltpu.VMEM((HEADS_HERE, 2 * FRAME, PAIR), BF),
            pltpu.VMEM((BLOCK, D), F32),
            dma((5,)),
            dma((2, 16)),
            dma((2, 16)),
            dma((4,)),
            dma((4,)),
            dma((3,)),
            dma((3,)),
            dma((24,)),
            dma((24,)),
            dma((2,)),
            dma((2,)),
        ],
        compiler_params=pltpu.CompilerParams(
            collective_id=0, has_side_effects=True, vmem_limit_bytes=56 * 1024 * 1024
        ),
        name="frame_attention_grad",
    )(latents, cotangent, norm_gain.reshape(1, D), jnp.transpose(w_qkv, (1, 0, 2)), w_out)


def solution(mesh):
    return jax.shard_map(
        shards,
        mesh=mesh,
        in_specs=(
            P(("tm", "head"), None),
            P(("tm", "head"), None),
            P(),
            P(None, None, "head"),
            P("head", None),
        ),
        out_specs=P(("tm", "head"), None),
        check_vma=False,
    )
```

```python
import functools

import jax
import jax.numpy as jnp
from jax import lax
from jax.experimental import pallas as pl
from jax.experimental.pallas import tpu as pltpu
from jax.sharding import PartitionSpec as P

EPSILON = 1e-06
MESH = pl.DeviceIdType.MESH
D = 3072
HEAD_DIM = 128
HEADS_HERE = 3
WIDTH = HEADS_HERE * HEAD_DIM
BLOCK = 64
HALF = BLOCK // 2
STEP = BLOCK // 4
FRAME = 512
PAIR = 2 * BLOCK
PARTS = 4
COLS = D // PARTS
N_TM = 32
X = 4
SCALE = HEAD_DIM ** (-0.5)
BF = jnp.bfloat16
F32 = jnp.float32


def nt(a, b):
    return lax.dot_general(a, b, (((1,), (1,)), ((), ())), preferred_element_type=F32)


def nn(a, b):
    return jnp.dot(a, b, preferred_element_type=F32)


def kernel(
    lat_h, cot_h, gain_h, wqkv_h, wout_h, out_ref,
    lat, gain, wq, wo, hid, cot, inv, q, kv, kt, probs, acc_k, acc_v, back_s, back_r, g,
    part, ra, rb, rl, rr, zs, rz, ga_s, ds_s, ga_f, ds_f, pb_f, grad,
    ld_sem, gs_sem, gr_sem, kvs_sem, kvr_sem, bs_sem, br_sem, rs_sem, rr_sem, zs_sem, zr_sem,
):
    tm = lax.axis_index("tm")
    head = lax.axis_index("head")
    x = lax.rem(head, X)
    base = head - x
    right = (tm, base + lax.rem(x + 1, X))
    left = (tm, base + lax.rem(x + X - 1, X))
    across = (tm, lax.rem(head + X, 2 * X))
    after = (lax.rem(tm + 1, N_TM), head)
    before = (lax.rem(tm + N_TM - 1, N_TM), head)

    barrier = pltpu.get_barrier_semaphore()
    for peer in (right, left, across, after, before):
        pl.semaphore_signal(barrier, inc=1, device_id=peer, device_id_type=MESH)

    loads = [
        pltpu.make_async_copy(lat_h, lat, ld_sem.at[0]),
        pltpu.make_async_copy(gain_h, gain, ld_sem.at[1]),
        pltpu.make_async_copy(cot_h, cot.at[pl.ds(0, BLOCK)], ld_sem.at[2]),
        pltpu.make_async_copy(wqkv_h, wq, ld_sem.at[3]),
        pltpu.make_async_copy(wout_h, wo, ld_sem.at[4]),
    ]
    for load in loads:
        load.start()
    loads[0].wait()
    loads[1].wait()
    for r in range(4):
        rows = pl.ds(r * 16, 16)
        lf = lat[rows].astype(F32)
        scale = lax.rsqrt(jnp.mean(lf * lf, axis=-1, keepdims=True) + EPSILON)
        inv[rows] = jnp.broadcast_to(scale, (16, 128))
        hid[rows] = (lf * scale * gain[...]).astype(BF)
    pl.semaphore_wait(barrier, 5)

    sent = []

    def push(src, dst, s_sem, r_sem, peer):
        copy = pltpu.make_async_remote_copy(
            src_ref=src, dst_ref=dst, send_sem=s_sem, recv_sem=r_sem, device_id=peer, device_id_type=MESH
        )
        copy.start()
        sent.append(copy)
        return copy

    def chunk(slot, c):
        return pl.ds(slot * BLOCK + c * HALF, HALF)

    bufs = (hid, cot)
    moves = {}

    def gather_push(a, src_slot, dst_slot, c, peer):
        i = dst_slot * 4 + c
        moves[a, dst_slot, c] = push(
            bufs[a].at[pl.ds(src_slot * BLOCK + c * STEP, STEP)], bufs[a].at[pl.ds(dst_slot * BLOCK + c * STEP, STEP)],
            gs_sem.at[a, i], gr_sem.at[a, i], peer,
        )

    def got(a, slot, cs=(0, 1, 2, 3)):
        for c in cs:
            moves[a, slot, c].wait_recv()

    def to_right(a, zz, c):
        gather_push(a, 4 * zz, 4 * zz + 1, c, right)

    def to_left(a, zz, c):
        gather_push(a, 4 * zz, 4 * zz + 2, c, left)

    def spread(a, c):
        got(a, 4, (c,))
        to_right(a, 1, c)
        to_left(a, 1, c)

    def forward(a, zz, c):
        near = 4 * zz + 1 + c % 2
        got(a, near, (c,))
        gather_push(a, near, 4 * zz + 3, c, left if c % 2 else right)

    kv_copies = []

    def project(p):
        rows = pl.ds(p * PAIR, PAIR)
        h = hid[rows]
        q[rows] = nn(h, wq[0]).astype(BF)
        kv[rows, pl.ds(0, WIDTH)] = nn(h, wq[1]).astype(BF)
        kv[rows, pl.ds(WIDTH, WIDTH)] = nn(h, wq[2]).astype(BF)
        kv_copies.append(
            push(kv.at[rows], kv.at[pl.ds(FRAME + p * PAIR, PAIR)], kvs_sem.at[p], kvr_sem.at[p], after)
        )

    for c in range(4):
        gather_push(0, 0, 4, c, across)
        to_right(0, 0, (0, 2, 1, 3)[c])
        to_left(0, 0, (1, 3, 0, 2)[c])
    loads[2].wait()
    for c in range(4):
        forward(0, 0, c)
        (to_left if c % 2 else to_right)(1, 0, c)
    loads[3].wait()
    got(0, 1, (1, 3))
    project(0)
    spread(0, 0)
    spread(0, 1)
    got(0, 2, (0, 2))
    got(0, 3)
    project(1)
    spread(0, 2)
    for c in range(4):
        gather_push(1, 0, 4, c, across)
    spread(0, 3)
    for c in range(4):
        forward(0, 1, c)
    for c in range(4):
        (to_right if c % 2 else to_left)(1, 0, c)
    got(0, 5, (1, 3))
    project(2)
    for c in range(4):
        forward(1, 0, c)
    spread(1, 0)
    got(0, 6, (0, 2))
    got(0, 7)
    project(3)
    spread(1, 1)
    loads[4].wait()

    def lanes(h):
        return pl.ds(pl.multiple_of(h * HEAD_DIM, HEAD_DIM), HEAD_DIM)

    def v_lanes(h):
        return pl.ds(pl.multiple_of(WIDTH + h * HEAD_DIM, HEAD_DIM), HEAD_DIM)

    for copy in kv_copies:
        copy.wait_recv()

    def turn(h, carry):
        kt[h] = kv[:, lanes(h)].astype(F32).T.astype(BF)
        return carry

    lax.fori_loop(0, HEADS_HERE, turn, 0)

    def score(i, carry):
        p = i // HEADS_HERE
        h = i - p * HEADS_HERE
        rows = pl.ds(pl.multiple_of(p * PAIR, PAIR), PAIR)
        qh = q[rows, lanes(h)]
        own = nt(kv[pl.ds(0, FRAME), lanes(h)], qh) * SCALE
        prev = nt(kv[pl.ds(FRAME, FRAME), lanes(h)], qh) * SCALE
        prev = jnp.where(tm > 0, prev, -1e30)
        top = jnp.maximum(jnp.max(own, axis=0, keepdims=True), jnp.max(prev, axis=0, keepdims=True))
        own = jnp.exp(own - top)
        prev = jnp.exp(prev - top)
        total = jnp.sum(own, axis=0, keepdims=True) + jnp.sum(prev, axis=0, keepdims=True)
        part_of = 1.0 / total
        probs[i, pl.ds(0, FRAME)] = own * part_of
        probs[i, pl.ds(FRAME, FRAME)] = prev * part_of
        return carry

    lax.fori_loop(0, 2 * HEADS_HERE, score, 0)
    spread(1, 2)
    forward(1, 1, 0)
    forward(1, 1, 1)
    lax.fori_loop(2 * HEADS_HERE, 4 * HEADS_HERE, score, 0)

    def score_grads(p, h):
        pt = probs[p * HEADS_HERE + h]
        dp = nt(kv[:, v_lanes(h)], ga_s[:, lanes(h)])
        delta = jnp.sum(pt * dp, axis=0, keepdims=True)
        return pt, (pt * (dp - delta) * SCALE).astype(BF)

    def backward(p):
        rows = pl.ds(p * PAIR, PAIR)
        ga_s[...] = nt(cot[rows], wo[...]).astype(BF)

        def one(h, carry):
            pt, ds = score_grads(p, h)
            acc_k[:, lanes(h)] += nn(ds, q[rows, lanes(h)])
            acc_v[:, lanes(h)] += nn(pt.astype(BF), ga_s[:, lanes(h)])
            g[rows, lanes(h)] = nn(kt[h], ds).T.astype(BF)
            return carry

        lax.fori_loop(0, HEADS_HERE, one, 0)


    def backward_first():
        for p in (0, 1):
            ga_f[pl.ds(p * PAIR, PAIR)] = nt(cot[pl.ds(p * PAIR, PAIR)], wo[...]).astype(BF)

        def one(h, carry):
            rows = pl.ds(0, 2 * PAIR)
            dp = nt(kv[:, v_lanes(h)], ga_f[:, lanes(h)])
            for p in (0, 1):
                pt = probs[p * HEADS_HERE + h]
                dpp = dp[:, p * PAIR : (p + 1) * PAIR]
                delta = jnp.sum(pt * dpp, axis=0, keepdims=True)
                ds_f[:, pl.ds(p * PAIR, PAIR)] = (pt * (dpp - delta) * SCALE).astype(BF)
                pb_f[:, pl.ds(p * PAIR, PAIR)] = pt.astype(BF)
            acc_k[:, lanes(h)] = nn(ds_f[...], q[rows, lanes(h)])
            acc_v[:, lanes(h)] = nn(pb_f[...], ga_f[:, lanes(h)])
            g[rows, lanes(h)] = nn(kt[h], ds_f[...]).T.astype(BF)
            return carry

        lax.fori_loop(0, HEADS_HERE, one, 0)

    spread(1, 3)
    got(1, 1, (1, 3))
    got(1, 2, (0, 2))
    got(1, 3)
    backward_first()
    forward(1, 1, 2)
    forward(1, 1, 3)
    got(1, 5, (1, 3))
    backward(2)
    got(1, 6, (0, 2))
    got(1, 7)

    last = pl.ds(3 * PAIR, PAIR)
    own = pl.ds(0, FRAME)
    prev = pl.ds(FRAME, FRAME)
    ga_s[...] = nt(cot[last], wo[...]).astype(BF)

    def last_prev(h, carry):
        pt, ds = score_grads(3, h)
        ds_s[h] = ds
        back_s[:, lanes(h)] = (acc_k[prev, lanes(h)] + nn(ds[FRAME:], q[last, lanes(h)])).astype(BF)
        back_s[:, v_lanes(h)] = (acc_v[prev, lanes(h)] + nn(pt[FRAME:].astype(BF), ga_s[:, lanes(h)])).astype(BF)
        return carry

    lax.fori_loop(0, HEADS_HERE, last_prev, 0)
    pieces = ((448, 64), (256, 192), (0, 256))
    backs = []
    for i, (start, size) in enumerate(pieces):
        rows = pl.ds(start, size)
        backs.append(push(back_s.at[rows], back_r.at[rows], bs_sem.at[i], br_sem.at[i], before))

    def last_own(h, carry):
        g[last, lanes(h)] = nn(kt[h], ds_s[h]).T.astype(BF)
        acc_k[own, lanes(h)] += nn(ds_s[h, own], q[last, lanes(h)])
        acc_v[own, lanes(h)] += nn(probs[3 * HEADS_HERE + h, own].astype(BF), ga_s[:, lanes(h)])
        return carry

    lax.fori_loop(0, HEADS_HERE, last_own, 0)

    def join(i):
        rows = pl.ds(*pieces[i])
        backs[i].wait_recv()
        g[rows, pl.ds(WIDTH, WIDTH)] = (acc_k[rows] + back_r[rows, pl.ds(0, WIDTH)].astype(F32)).astype(BF)
        g[rows, pl.ds(2 * WIDTH, WIDTH)] = (acc_v[rows] + back_r[rows, pl.ds(WIDTH, WIDTH)].astype(F32)).astype(BF)

    def partials(i, hf):
        rows = pl.ds(*pieces[i])

        def tile(n, carry):
            w_rows = pl.ds(pl.multiple_of(hf * COLS + n * 384, 128), 384)
            total = nt(g[rows, pl.ds(0, WIDTH)], wq[0, w_rows])
            total += nt(g[rows, pl.ds(WIDTH, WIDTH)], wq[1, w_rows])
            total += nt(g[rows, pl.ds(2 * WIDTH, WIDTH)], wq[2, w_rows])
            part[hf, rows, pl.ds(pl.multiple_of(n * 384, 128), 384)] = total.astype(BF)
            return carry

        lax.fori_loop(0, COLS // 384, tile, 0)

    sums = {}

    def sum_push(key, i, src, dst, peer):
        zz, hf = key
        k = (zz * PARTS + hf) * 6 + i
        sums[key, i] = push(src, dst, rs_sem.at[k], rr_sem.at[k], peer)

    def opposite(zz, hf):
        u = zz * PARTS + hf
        sum_push((zz, hf), 0, part.at[hf, chunk(4 * zz + 3, 0)], ra.at[u], right)
        sum_push((zz, hf), 1, part.at[hf, chunk(4 * zz + 3, 1)], rb.at[u], left)

    def singles(zz, hf):
        u = zz * PARTS + hf
        sum_push((zz, hf), 2, part.at[hf, chunk(4 * zz + 2, 1)], rl.at[u, pl.ds(HALF, HALF)], right)
        sum_push((zz, hf), 3, part.at[hf, chunk(4 * zz + 1, 0)], rr.at[u, pl.ds(0, HALF)], left)

    def doubles(zz, hf):
        u = zz * PARTS + hf
        for_right = chunk(4 * zz + 2, 0)
        for_left = chunk(4 * zz + 1, 1)
        sums[(zz, hf), 0].wait_recv()
        part[hf, for_right] = (part[hf, for_right].astype(F32) + ra[u].astype(F32)).astype(BF)
        sum_push((zz, hf), 4, part.at[hf, for_right], rl.at[u, pl.ds(0, HALF)], right)
        sums[(zz, hf), 1].wait_recv()
        part[hf, for_left] = (part[hf, for_left].astype(F32) + rb[u].astype(F32)).astype(BF)
        sum_push((zz, hf), 5, part.at[hf, for_left], rr.at[u, pl.ds(HALF, HALF)], left)

    crossing = {}

    def cross(hf):
        for i in (2, 3, 4, 5):
            sums[(1, hf), i].wait_recv()
        mine = part[hf, pl.ds(256, BLOCK)].astype(F32)
        zs[hf] = (mine + rl[PARTS + hf].astype(F32) + rr[PARTS + hf].astype(F32)).astype(BF)
        crossing[hf] = push(zs.at[hf], rz.at[hf], zs_sem.at[hf], zr_sem.at[hf], across)

    join(0)
    for hf in range(PARTS):
        partials(0, hf)
        opposite(1, hf)
    join(1)
    for hf in range(PARTS):
        partials(1, hf)
        singles(1, hf)
        doubles(1, hf)
        if hf:
            cross(hf - 1)
    join(2)
    for hf in range(PARTS):
        partials(2, hf)
        opposite(0, hf)
        singles(0, hf)
        if hf:
            doubles(0, hf - 1)
        else:
            cross(PARTS - 1)
    doubles(0, PARTS - 1)
    for hf in range(PARTS):
        for i in (2, 3, 4, 5):
            sums[(0, hf), i].wait_recv()
    for hf in range(PARTS):
        crossing[hf].wait_recv()

    for r in range(4):
        rows = pl.ds(r * 16, 16)
        scale = inv[rows, pl.ds(0, 1)]
        inner = jnp.zeros((16, 1), F32)
        for hf in range(PARTS):
            cols = pl.ds(hf * COLS, COLS)
            total = (
                part[hf, rows].astype(F32) + rl[hf, rows].astype(F32) + rr[hf, rows].astype(F32)
                + rz[hf, rows].astype(F32)
            )
            total = total * gain[:, cols]
            inner += jnp.sum(total * (lat[rows, cols].astype(F32) * scale), axis=-1, keepdims=True)
            grad[rows, cols] = total
        inner = inner * (1.0 / D)
        normed = lat[rows].astype(F32) * scale
        out_ref[rows] = (cot[rows].astype(F32) + scale * (grad[rows] - normed * inner)).astype(BF)

    for copy in sent:
        copy.wait_send()


def shards(latents, cotangent, norm_gain, w_qkv, w_out):
    hbm = pl.BlockSpec(memory_space=pl.ANY)
    dma = pltpu.SemaphoreType.DMA
    return pl.pallas_call(
        kernel,
        out_shape=jax.ShapeDtypeStruct((BLOCK, D), BF),
        in_specs=[hbm] * 5,
        out_specs=pl.BlockSpec(memory_space=pltpu.VMEM),
        scratch_shapes=[
            pltpu.VMEM((BLOCK, D), BF),
            pltpu.VMEM((1, D), F32),
            pltpu.VMEM((3, D, WIDTH), BF),
            pltpu.VMEM((WIDTH, D), BF),
            pltpu.VMEM((FRAME, D), BF),
            pltpu.VMEM((FRAME, D), BF),
            pltpu.VMEM((BLOCK, 128), F32),
            pltpu.VMEM((FRAME, WIDTH), BF),
            pltpu.VMEM((2 * FRAME, 2 * WIDTH), BF),
            pltpu.VMEM((HEADS_HERE, HEAD_DIM, 2 * FRAME), BF),
            pltpu.VMEM((4 * HEADS_HERE, 2 * FRAME, PAIR), F32),
            pltpu.VMEM((2 * FRAME, WIDTH), F32),
            pltpu.VMEM((2 * FRAME, WIDTH), F32),
            pltpu.VMEM((FRAME, 2 * WIDTH), BF),
            pltpu.VMEM((FRAME, 2 * WIDTH), BF),
            pltpu.VMEM((FRAME, 3 * WIDTH), BF),
            pltpu.VMEM((PARTS, FRAME, COLS), BF),
            pltpu.VMEM((2 * PARTS, HALF, COLS), BF),
            pltpu.VMEM((2 * PARTS, HALF, COLS), BF),
            pltpu.VMEM((2 * PARTS, BLOCK, COLS), BF),
            pltpu.VMEM((2 * PARTS, BLOCK, COLS), BF),
            pltpu.VMEM((PARTS, BLOCK, COLS), BF),
            pltpu.VMEM((PARTS, BLOCK, COLS), BF),
            pltpu.VMEM((PAIR, WIDTH), BF),
            pltpu.VMEM((HEADS_HERE, 2 * FRAME, PAIR), BF),
            pltpu.VMEM((2 * PAIR, WIDTH), BF),
            pltpu.VMEM((2 * FRAME, 2 * PAIR), BF),
            pltpu.VMEM((2 * FRAME, 2 * PAIR), BF),
            pltpu.VMEM((BLOCK, D), F32),
            dma((5,)),
            dma((2, 32)),
            dma((2, 32)),
            dma((4,)),
            dma((4,)),
            dma((3,)),
            dma((3,)),
            dma((12 * PARTS,)),
            dma((12 * PARTS,)),
            dma((PARTS,)),
            dma((PARTS,)),
        ],
        compiler_params=pltpu.CompilerParams(
            collective_id=0, has_side_effects=True, vmem_limit_bytes=56 * 1024 * 1024
        ),
        name="frame_attention_grad",
    )(latents, cotangent, norm_gain.reshape(1, D), jnp.transpose(w_qkv, (1, 0, 2)), w_out)


def solution(mesh):
    return jax.shard_map(
        shards,
        mesh=mesh,
        in_specs=(
            P(("tm", "head"), None),
            P(("tm", "head"), None),
            P(),
            P(None, None, "head"),
            P("head", None),
        ),
        out_specs=P(("tm", "head"), None),
        check_vma=False,
    )
```

```python
import functools

import jax
import jax.numpy as jnp
from jax import lax
from jax.experimental import pallas as pl
from jax.experimental.pallas import tpu as pltpu
from jax.sharding import PartitionSpec as P

EPSILON = 1e-06
MESH = pl.DeviceIdType.MESH
D = 3072
HEAD_DIM = 128
HEADS_HERE = 3
WIDTH = HEADS_HERE * HEAD_DIM
BLOCK = 64
HALF = BLOCK // 2
STEP = BLOCK // 4
FRAME = 512
PAIR = 2 * BLOCK
PARTS = 4
COLS = D // PARTS
N_TM = 32
X = 4
SCALE = HEAD_DIM ** (-0.5)
BF = jnp.bfloat16
F32 = jnp.float32


def nt(a, b):
    return lax.dot_general(a, b, (((1,), (1,)), ((), ())), preferred_element_type=F32)


def nn(a, b):
    return jnp.dot(a, b, preferred_element_type=F32)


def kernel(
    lat_h, cot_h, gain_h, wqkv_h, wout_h, out_ref,
    lat, gain, wq, wo, hid, cot, inv, q, kv, kt, probs, acc_k, acc_v, back_s, back_r, g,
    part, ra, rb, rl, rr, zs, rz, ga_s, ds_s, ga_f, ds_f, pb_f, grad,
    ld_sem, gs_sem, gr_sem, kvs_sem, kvr_sem, bs_sem, br_sem, rs_sem, rr_sem, zs_sem, zr_sem,
):
    tm = lax.axis_index("tm")
    head = lax.axis_index("head")
    x = lax.rem(head, X)
    base = head - x
    right = (tm, base + lax.rem(x + 1, X))
    left = (tm, base + lax.rem(x + X - 1, X))
    across = (tm, lax.rem(head + X, 2 * X))
    after = (lax.rem(tm + 1, N_TM), head)
    before = (lax.rem(tm + N_TM - 1, N_TM), head)

    barrier = pltpu.get_barrier_semaphore()
    for peer in (right, left, across, after, before):
        pl.semaphore_signal(barrier, inc=1, device_id=peer, device_id_type=MESH)

    loads = [
        pltpu.make_async_copy(lat_h, lat, ld_sem.at[0]),
        pltpu.make_async_copy(gain_h, gain, ld_sem.at[1]),
        pltpu.make_async_copy(cot_h, cot.at[pl.ds(0, BLOCK)], ld_sem.at[2]),
        pltpu.make_async_copy(wqkv_h, wq, ld_sem.at[3]),
        pltpu.make_async_copy(wout_h, wo, ld_sem.at[4]),
    ]
    for load in loads:
        load.start()
    loads[0].wait()
    loads[1].wait()
    for r in range(4):
        rows = pl.ds(r * 16, 16)
        lf = lat[rows].astype(F32)
        scale = lax.rsqrt(jnp.mean(lf * lf, axis=-1, keepdims=True) + EPSILON)
        inv[rows] = jnp.broadcast_to(scale, (16, 128))
        hid[rows] = (lf * scale * gain[...]).astype(BF)
    pl.semaphore_wait(barrier, 5)

    sent = []

    def push(src, dst, s_sem, r_sem, peer):
        copy = pltpu.make_async_remote_copy(
            src_ref=src, dst_ref=dst, send_sem=s_sem, recv_sem=r_sem, device_id=peer, device_id_type=MESH
        )
        copy.start()
        sent.append(copy)
        return copy

    def chunk(slot, c):
        return pl.ds(slot * BLOCK + c * HALF, HALF)

    bufs = (hid, cot)
    moves = {}

    def gather_push(a, src_slot, dst_slot, c, peer):
        i = dst_slot * 4 + c
        moves[a, dst_slot, c] = push(
            bufs[a].at[pl.ds(src_slot * BLOCK + c * STEP, STEP)], bufs[a].at[pl.ds(dst_slot * BLOCK + c * STEP, STEP)],
            gs_sem.at[a, i], gr_sem.at[a, i], peer,
        )

    def got(a, slot, cs=(0, 1, 2, 3)):
        for c in cs:
            moves[a, slot, c].wait_recv()

    def to_right(a, zz, c):
        gather_push(a, 4 * zz, 4 * zz + 1, c, right)

    def to_left(a, zz, c):
        gather_push(a, 4 * zz, 4 * zz + 2, c, left)

    def spread(a, c):
        got(a, 4, (c,))
        to_right(a, 1, c)
        to_left(a, 1, c)

    def forward(a, zz, c):
        near = 4 * zz + 1 + c % 2
        got(a, near, (c,))
        gather_push(a, near, 4 * zz + 3, c, left if c % 2 else right)

    kv_copies = []

    def project(p):
        rows = pl.ds(p * PAIR, PAIR)
        h = hid[rows]
        q[rows] = nn(h, wq[0]).astype(BF)
        kv[rows, pl.ds(0, WIDTH)] = nn(h, wq[1]).astype(BF)
        kv[rows, pl.ds(WIDTH, WIDTH)] = nn(h, wq[2]).astype(BF)
        kv_copies.append(
            push(kv.at[rows], kv.at[pl.ds(FRAME + p * PAIR, PAIR)], kvs_sem.at[p], kvr_sem.at[p], after)
        )

    for c in range(4):
        gather_push(0, 0, 4, c, across)
        to_right(0, 0, (0, 2, 1, 3)[c])
        to_left(0, 0, (1, 3, 0, 2)[c])
    loads[2].wait()
    for c in range(4):
        forward(0, 0, c)
        to_right(1, 0, (0, 2, 1, 3)[c])
        to_left(1, 0, (1, 3, 0, 2)[c])
    loads[3].wait()
    got(0, 1, (1, 3))
    project(0)
    spread(0, 0)
    spread(0, 1)
    got(0, 2, (0, 2))
    got(0, 3)
    project(1)
    for c in range(4):
        forward(1, 0, c)
    spread(0, 2)
    for c in range(4):
        gather_push(1, 0, 4, c, across)
    spread(0, 3)
    for c in range(4):
        forward(0, 1, c)
    got(0, 5, (1, 3))
    project(2)
    spread(1, 0)
    got(0, 6, (0, 2))
    got(0, 7)
    project(3)
    spread(1, 1)
    loads[4].wait()

    def lanes(h):
        return pl.ds(pl.multiple_of(h * HEAD_DIM, HEAD_DIM), HEAD_DIM)

    def v_lanes(h):
        return pl.ds(pl.multiple_of(WIDTH + h * HEAD_DIM, HEAD_DIM), HEAD_DIM)

    for copy in kv_copies:
        copy.wait_recv()

    def turn(h, carry):
        kt[h] = kv[:, lanes(h)].astype(F32).T.astype(BF)
        return carry

    lax.fori_loop(0, HEADS_HERE, turn, 0)

    def score(i, carry):
        p = i // HEADS_HERE
        h = i - p * HEADS_HERE
        rows = pl.ds(pl.multiple_of(p * PAIR, PAIR), PAIR)
        qh = q[rows, lanes(h)]
        own = nt(kv[pl.ds(0, FRAME), lanes(h)], qh) * SCALE
        prev = nt(kv[pl.ds(FRAME, FRAME), lanes(h)], qh) * SCALE
        prev = jnp.where(tm > 0, prev, -1e30)
        top = jnp.maximum(jnp.max(own, axis=0, keepdims=True), jnp.max(prev, axis=0, keepdims=True))
        own = jnp.exp(own - top)
        prev = jnp.exp(prev - top)
        total = jnp.sum(own, axis=0, keepdims=True) + jnp.sum(prev, axis=0, keepdims=True)
        part_of = 1.0 / total
        probs[i, pl.ds(0, FRAME)] = own * part_of
        probs[i, pl.ds(FRAME, FRAME)] = prev * part_of
        return carry

    lax.fori_loop(0, 2 * HEADS_HERE, score, 0)
    spread(1, 2)
    forward(1, 1, 0)
    forward(1, 1, 1)
    lax.fori_loop(2 * HEADS_HERE, 4 * HEADS_HERE, score, 0)

    def score_grads(p, h):
        pt = probs[p * HEADS_HERE + h]
        dp = nt(kv[:, v_lanes(h)], ga_s[:, lanes(h)])
        delta = jnp.sum(pt * dp, axis=0, keepdims=True)
        return pt, (pt * (dp - delta) * SCALE).astype(BF)

    def backward(p):
        rows = pl.ds(p * PAIR, PAIR)
        ga_s[...] = nt(cot[rows], wo[...]).astype(BF)

        def one(h, carry):
            pt, ds = score_grads(p, h)
            acc_k[:, lanes(h)] += nn(ds, q[rows, lanes(h)])
            acc_v[:, lanes(h)] += nn(pt.astype(BF), ga_s[:, lanes(h)])
            g[rows, lanes(h)] = nn(kt[h], ds).T.astype(BF)
            return carry

        lax.fori_loop(0, HEADS_HERE, one, 0)


    def backward_first():
        for p in (0, 1):
            ga_f[pl.ds(p * PAIR, PAIR)] = nt(cot[pl.ds(p * PAIR, PAIR)], wo[...]).astype(BF)

        def one(h, carry):
            rows = pl.ds(0, 2 * PAIR)
            dp = nt(kv[:, v_lanes(h)], ga_f[:, lanes(h)])
            for p in (0, 1):
                pt = probs[p * HEADS_HERE + h]
                dpp = dp[:, p * PAIR : (p + 1) * PAIR]
                delta = jnp.sum(pt * dpp, axis=0, keepdims=True)
                ds_f[:, pl.ds(p * PAIR, PAIR)] = (pt * (dpp - delta) * SCALE).astype(BF)
                pb_f[:, pl.ds(p * PAIR, PAIR)] = pt.astype(BF)
            acc_k[:, lanes(h)] = nn(ds_f[...], q[rows, lanes(h)])
            acc_v[:, lanes(h)] = nn(pb_f[...], ga_f[:, lanes(h)])
            g[rows, lanes(h)] = nn(kt[h], ds_f[...]).T.astype(BF)
            return carry

        lax.fori_loop(0, HEADS_HERE, one, 0)

    spread(1, 3)
    got(1, 1, (1, 3))
    got(1, 2, (0, 2))
    got(1, 3)
    backward_first()
    forward(1, 1, 2)
    forward(1, 1, 3)
    got(1, 5, (1, 3))
    backward(2)
    got(1, 6, (0, 2))
    got(1, 7)

    last = pl.ds(3 * PAIR, PAIR)
    own = pl.ds(0, FRAME)
    prev = pl.ds(FRAME, FRAME)
    ga_s[...] = nt(cot[last], wo[...]).astype(BF)

    def last_prev(h, carry):
        pt, ds = score_grads(3, h)
        ds_s[h] = ds
        back_s[:, lanes(h)] = (acc_k[prev, lanes(h)] + nn(ds[FRAME:], q[last, lanes(h)])).astype(BF)
        back_s[:, v_lanes(h)] = (acc_v[prev, lanes(h)] + nn(pt[FRAME:].astype(BF), ga_s[:, lanes(h)])).astype(BF)
        return carry

    lax.fori_loop(0, HEADS_HERE, last_prev, 0)
    pieces = ((448, 64), (256, 192), (0, 256))
    backs = []
    for i, (start, size) in enumerate(pieces):
        rows = pl.ds(start, size)
        backs.append(push(back_s.at[rows], back_r.at[rows], bs_sem.at[i], br_sem.at[i], before))

    def last_own(h, carry):
        g[last, lanes(h)] = nn(kt[h], ds_s[h]).T.astype(BF)
        acc_k[own, lanes(h)] += nn(ds_s[h, own], q[last, lanes(h)])
        acc_v[own, lanes(h)] += nn(probs[3 * HEADS_HERE + h, own].astype(BF), ga_s[:, lanes(h)])
        return carry

    lax.fori_loop(0, HEADS_HERE, last_own, 0)

    def join(i):
        rows = pl.ds(*pieces[i])
        backs[i].wait_recv()
        g[rows, pl.ds(WIDTH, WIDTH)] = (acc_k[rows] + back_r[rows, pl.ds(0, WIDTH)].astype(F32)).astype(BF)
        g[rows, pl.ds(2 * WIDTH, WIDTH)] = (acc_v[rows] + back_r[rows, pl.ds(WIDTH, WIDTH)].astype(F32)).astype(BF)

    def partials(i, hf):
        rows = pl.ds(*pieces[i])

        def tile(n, carry):
            w_rows = pl.ds(pl.multiple_of(hf * COLS + n * 384, 128), 384)
            total = nt(g[rows, pl.ds(0, WIDTH)], wq[0, w_rows])
            total += nt(g[rows, pl.ds(WIDTH, WIDTH)], wq[1, w_rows])
            total += nt(g[rows, pl.ds(2 * WIDTH, WIDTH)], wq[2, w_rows])
            part[hf, rows, pl.ds(pl.multiple_of(n * 384, 128), 384)] = total.astype(BF)
            return carry

        lax.fori_loop(0, COLS // 384, tile, 0)

    sums = {}

    def sum_push(key, i, src, dst, peer):
        zz, hf = key
        k = (zz * PARTS + hf) * 6 + i
        sums[key, i] = push(src, dst, rs_sem.at[k], rr_sem.at[k], peer)

    def opposite(zz, hf):
        u = zz * PARTS + hf
        sum_push((zz, hf), 0, part.at[hf, chunk(4 * zz + 3, 0)], ra.at[u], right)
        sum_push((zz, hf), 1, part.at[hf, chunk(4 * zz + 3, 1)], rb.at[u], left)

    def singles(zz, hf):
        u = zz * PARTS + hf
        sum_push((zz, hf), 2, part.at[hf, chunk(4 * zz + 2, 1)], rl.at[u, pl.ds(HALF, HALF)], right)
        sum_push((zz, hf), 3, part.at[hf, chunk(4 * zz + 1, 0)], rr.at[u, pl.ds(0, HALF)], left)

    def doubles(zz, hf):
        u = zz * PARTS + hf
        for_right = chunk(4 * zz + 2, 0)
        for_left = chunk(4 * zz + 1, 1)
        sums[(zz, hf), 0].wait_recv()
        part[hf, for_right] = (part[hf, for_right].astype(F32) + ra[u].astype(F32)).astype(BF)
        sum_push((zz, hf), 4, part.at[hf, for_right], rl.at[u, pl.ds(0, HALF)], right)
        sums[(zz, hf), 1].wait_recv()
        part[hf, for_left] = (part[hf, for_left].astype(F32) + rb[u].astype(F32)).astype(BF)
        sum_push((zz, hf), 5, part.at[hf, for_left], rr.at[u, pl.ds(HALF, HALF)], left)

    crossing = {}

    def cross(hf):
        for i in (2, 3, 4, 5):
            sums[(1, hf), i].wait_recv()
        mine = part[hf, pl.ds(256, BLOCK)].astype(F32)
        zs[hf] = (mine + rl[PARTS + hf].astype(F32) + rr[PARTS + hf].astype(F32)).astype(BF)
        crossing[hf] = push(zs.at[hf], rz.at[hf], zs_sem.at[hf], zr_sem.at[hf], across)

    join(0)
    for hf in range(PARTS):
        partials(0, hf)
        opposite(1, hf)
    join(1)
    for hf in range(PARTS):
        partials(1, hf)
        singles(1, hf)
        doubles(1, hf)
    join(2)
    for hf in range(PARTS):
        partials(2, hf)
        opposite(0, hf)
        singles(0, hf)
        cross(hf)
    for hf in range(PARTS):
        doubles(0, hf)
    for hf in range(PARTS):
        for i in (2, 3, 4, 5):
            sums[(0, hf), i].wait_recv()
    for hf in range(PARTS):
        crossing[hf].wait_recv()

    for r in range(4):
        rows = pl.ds(r * 16, 16)
        scale = inv[rows, pl.ds(0, 1)]
        inner = jnp.zeros((16, 1), F32)
        for hf in range(PARTS):
            cols = pl.ds(hf * COLS, COLS)
            total = (
                part[hf, rows].astype(F32) + rl[hf, rows].astype(F32) + rr[hf, rows].astype(F32)
                + rz[hf, rows].astype(F32)
            )
            total = total * gain[:, cols]
            inner += jnp.sum(total * (lat[rows, cols].astype(F32) * scale), axis=-1, keepdims=True)
            grad[rows, cols] = total
        inner = inner * (1.0 / D)
        normed = lat[rows].astype(F32) * scale
        out_ref[rows] = (cot[rows].astype(F32) + scale * (grad[rows] - normed * inner)).astype(BF)

    for copy in sent:
        copy.wait_send()


def shards(latents, cotangent, norm_gain, w_qkv, w_out):
    hbm = pl.BlockSpec(memory_space=pl.ANY)
    dma = pltpu.SemaphoreType.DMA
    return pl.pallas_call(
        kernel,
        out_shape=jax.ShapeDtypeStruct((BLOCK, D), BF),
        in_specs=[hbm] * 5,
        out_specs=pl.BlockSpec(memory_space=pltpu.VMEM),
        scratch_shapes=[
            pltpu.VMEM((BLOCK, D), BF),
            pltpu.VMEM((1, D), F32),
            pltpu.VMEM((3, D, WIDTH), BF),
            pltpu.VMEM((WIDTH, D), BF),
            pltpu.VMEM((FRAME, D), BF),
            pltpu.VMEM((FRAME, D), BF),
            pltpu.VMEM((BLOCK, 128), F32),
            pltpu.VMEM((FRAME, WIDTH), BF),
            pltpu.VMEM((2 * FRAME, 2 * WIDTH), BF),
            pltpu.VMEM((HEADS_HERE, HEAD_DIM, 2 * FRAME), BF),
            pltpu.VMEM((4 * HEADS_HERE, 2 * FRAME, PAIR), F32),
            pltpu.VMEM((2 * FRAME, WIDTH), F32),
            pltpu.VMEM((2 * FRAME, WIDTH), F32),
            pltpu.VMEM((FRAME, 2 * WIDTH), BF),
            pltpu.VMEM((FRAME, 2 * WIDTH), BF),
            pltpu.VMEM((FRAME, 3 * WIDTH), BF),
            pltpu.VMEM((PARTS, FRAME, COLS), BF),
            pltpu.VMEM((2 * PARTS, HALF, COLS), BF),
            pltpu.VMEM((2 * PARTS, HALF, COLS), BF),
            pltpu.VMEM((2 * PARTS, BLOCK, COLS), BF),
            pltpu.VMEM((2 * PARTS, BLOCK, COLS), BF),
            pltpu.VMEM((PARTS, BLOCK, COLS), BF),
            pltpu.VMEM((PARTS, BLOCK, COLS), BF),
            pltpu.VMEM((PAIR, WIDTH), BF),
            pltpu.VMEM((HEADS_HERE, 2 * FRAME, PAIR), BF),
            pltpu.VMEM((2 * PAIR, WIDTH), BF),
            pltpu.VMEM((2 * FRAME, 2 * PAIR), BF),
            pltpu.VMEM((2 * FRAME, 2 * PAIR), BF),
            pltpu.VMEM((BLOCK, D), F32),
            dma((5,)),
            dma((2, 32)),
            dma((2, 32)),
            dma((4,)),
            dma((4,)),
            dma((3,)),
            dma((3,)),
            dma((12 * PARTS,)),
            dma((12 * PARTS,)),
            dma((PARTS,)),
            dma((PARTS,)),
        ],
        compiler_params=pltpu.CompilerParams(
            collective_id=0, has_side_effects=True, vmem_limit_bytes=56 * 1024 * 1024
        ),
        name="frame_attention_grad",
    )(latents, cotangent, norm_gain.reshape(1, D), jnp.transpose(w_qkv, (1, 0, 2)), w_out)


def solution(mesh):
    return jax.shard_map(
        shards,
        mesh=mesh,
        in_specs=(
            P(("tm", "head"), None),
            P(("tm", "head"), None),
            P(),
            P(None, None, "head"),
            P("head", None),
        ),
        out_specs=P(("tm", "head"), None),
        check_vma=False,
    )
```

```python
import functools

import jax
import jax.numpy as jnp
from jax import lax
from jax.experimental import pallas as pl
from jax.experimental.pallas import tpu as pltpu
from jax.sharding import PartitionSpec as P

EPSILON = 1e-06
MESH = pl.DeviceIdType.MESH
D = 3072
HEAD_DIM = 128
HEADS_HERE = 3
WIDTH = HEADS_HERE * HEAD_DIM
BLOCK = 64
HALF = BLOCK // 2
STEP = BLOCK // 4
FRAME = 512
PAIR = 2 * BLOCK
PARTS = 4
COLS = D // PARTS
N_TM = 32
X = 4
SCALE = HEAD_DIM ** (-0.5)
BF = jnp.bfloat16
F32 = jnp.float32


def nt(a, b):
    return lax.dot_general(a, b, (((1,), (1,)), ((), ())), preferred_element_type=F32)


def nn(a, b):
    return jnp.dot(a, b, preferred_element_type=F32)


def kernel(
    lat_h, cot_h, gain_h, wqkv_h, wout_h, out_ref,
    lat, gain, wq, wo, hid, cot, inv, q, kv, kt, probs, acc_k, acc_v, back_s, back_r, g,
    part, ra, rb, rl, rr, zs, rz, ga_s, ds_s, ga_f, ds_f, pb_f, grad,
    ld_sem, gs_sem, gr_sem, kvs_sem, kvr_sem, bs_sem, br_sem, rs_sem, rr_sem, zs_sem, zr_sem,
):
    tm = lax.axis_index("tm")
    head = lax.axis_index("head")
    x = lax.rem(head, X)
    base = head - x
    right = (tm, base + lax.rem(x + 1, X))
    left = (tm, base + lax.rem(x + X - 1, X))
    across = (tm, lax.rem(head + X, 2 * X))
    after = (lax.rem(tm + 1, N_TM), head)
    before = (lax.rem(tm + N_TM - 1, N_TM), head)

    barrier = pltpu.get_barrier_semaphore()
    for peer in (right, left, across, after, before):
        pl.semaphore_signal(barrier, inc=1, device_id=peer, device_id_type=MESH)

    loads = [
        pltpu.make_async_copy(lat_h, lat, ld_sem.at[0]),
        pltpu.make_async_copy(gain_h, gain, ld_sem.at[1]),
        pltpu.make_async_copy(cot_h, cot.at[pl.ds(0, BLOCK)], ld_sem.at[2]),
        pltpu.make_async_copy(wqkv_h, wq, ld_sem.at[3]),
        pltpu.make_async_copy(wout_h, wo, ld_sem.at[4]),
    ]
    for load in loads:
        load.start()
    loads[0].wait()
    loads[1].wait()
    for r in range(4):
        rows = pl.ds(r * 16, 16)
        lf = lat[rows].astype(F32)
        scale = lax.rsqrt(jnp.mean(lf * lf, axis=-1, keepdims=True) + EPSILON)
        inv[rows] = jnp.broadcast_to(scale, (16, 128))
        hid[rows] = (lf * scale * gain[...]).astype(BF)
    pl.semaphore_wait(barrier, 5)

    sent = []

    def push(src, dst, s_sem, r_sem, peer):
        copy = pltpu.make_async_remote_copy(
            src_ref=src, dst_ref=dst, send_sem=s_sem, recv_sem=r_sem, device_id=peer, device_id_type=MESH
        )
        copy.start()
        sent.append(copy)
        return copy

    def chunk(slot, c):
        return pl.ds(slot * BLOCK + c * HALF, HALF)

    bufs = (hid, cot)
    moves = {}

    def gather_push(a, src_slot, dst_slot, c, peer):
        i = dst_slot * 4 + c
        moves[a, dst_slot, c] = push(
            bufs[a].at[pl.ds(src_slot * BLOCK + c * STEP, STEP)], bufs[a].at[pl.ds(dst_slot * BLOCK + c * STEP, STEP)],
            gs_sem.at[a, i], gr_sem.at[a, i], peer,
        )

    def got(a, slot, cs=(0, 1, 2, 3)):
        for c in cs:
            moves[a, slot, c].wait_recv()

    def to_right(a, zz, c):
        gather_push(a, 4 * zz, 4 * zz + 1, c, right)

    def to_left(a, zz, c):
        gather_push(a, 4 * zz, 4 * zz + 2, c, left)

    def spread(a, c):
        got(a, 4, (c,))
        to_right(a, 1, c)
        to_left(a, 1, c)

    def forward(a, zz, c):
        near = 4 * zz + 1 + c % 2
        got(a, near, (c,))
        gather_push(a, near, 4 * zz + 3, c, left if c % 2 else right)

    kv_copies = []

    def project(p):
        rows = pl.ds(p * PAIR, PAIR)
        h = hid[rows]
        q[rows] = nn(h, wq[0]).astype(BF)
        kv[rows, pl.ds(0, WIDTH)] = nn(h, wq[1]).astype(BF)
        kv[rows, pl.ds(WIDTH, WIDTH)] = nn(h, wq[2]).astype(BF)
        kv_copies.append(
            push(kv.at[rows], kv.at[pl.ds(FRAME + p * PAIR, PAIR)], kvs_sem.at[p], kvr_sem.at[p], after)
        )

    for c in range(4):
        gather_push(0, 0, 4, c, across)
        to_right(0, 0, (0, 2, 1, 3)[c])
        to_left(0, 0, (1, 3, 0, 2)[c])
    loads[2].wait()
    for c in range(4):
        forward(0, 0, c)
        to_right(1, 0, (0, 2, 1, 3)[c])
        to_left(1, 0, (1, 3, 0, 2)[c])
    loads[3].wait()
    got(0, 1, (1, 3))
    project(0)
    spread(0, 0)
    spread(0, 1)
    got(0, 2, (0, 2))
    got(0, 3)
    project(1)
    for c in range(4):
        gather_push(1, 0, 4, c, across)
    for c in range(4):
        forward(1, 0, c)
    spread(0, 2)
    spread(0, 3)
    for c in range(4):
        forward(0, 1, c)
    got(0, 5, (1, 3))
    project(2)
    spread(1, 0)
    got(0, 6, (0, 2))
    got(0, 7)
    project(3)
    spread(1, 1)
    loads[4].wait()

    def lanes(h):
        if isinstance(h, int):
            return pl.ds(h * HEAD_DIM, HEAD_DIM)
        return pl.ds(pl.multiple_of(h * HEAD_DIM, HEAD_DIM), HEAD_DIM)

    def v_lanes(h):
        if isinstance(h, int):
            return pl.ds(WIDTH + h * HEAD_DIM, HEAD_DIM)
        return pl.ds(pl.multiple_of(WIDTH + h * HEAD_DIM, HEAD_DIM), HEAD_DIM)

    for copy in kv_copies:
        copy.wait_recv()

    def turn(h, carry):
        kt[h] = kv[:, lanes(h)].astype(F32).T.astype(BF)
        return carry

    lax.fori_loop(0, HEADS_HERE, turn, 0)

    def score(i, carry):
        p = i // HEADS_HERE
        h = i - p * HEADS_HERE
        rows = pl.ds(pl.multiple_of(p * PAIR, PAIR), PAIR)
        qh = q[rows, lanes(h)]
        own = nt(kv[pl.ds(0, FRAME), lanes(h)], qh) * SCALE
        prev = nt(kv[pl.ds(FRAME, FRAME), lanes(h)], qh) * SCALE
        prev = jnp.where(tm > 0, prev, -1e30)
        top = jnp.maximum(jnp.max(own, axis=0, keepdims=True), jnp.max(prev, axis=0, keepdims=True))
        own = jnp.exp(own - top)
        prev = jnp.exp(prev - top)
        total = jnp.sum(own, axis=0, keepdims=True) + jnp.sum(prev, axis=0, keepdims=True)
        part_of = 1.0 / total
        probs[i, pl.ds(0, FRAME)] = own * part_of
        probs[i, pl.ds(FRAME, FRAME)] = prev * part_of
        return carry

    lax.fori_loop(0, 2 * HEADS_HERE, score, 0)
    spread(1, 2)
    lax.fori_loop(2 * HEADS_HERE, 4 * HEADS_HERE, score, 0)

    def score_grads(p, h):
        pt = probs[p * HEADS_HERE + h]
        dp = nt(kv[:, v_lanes(h)], ga_s[:, lanes(h)])
        delta = jnp.sum(pt * dp, axis=0, keepdims=True)
        return pt, (pt * (dp - delta) * SCALE).astype(BF)

    def backward(p):
        rows = pl.ds(p * PAIR, PAIR)
        ga_s[...] = nt(cot[rows], wo[...]).astype(BF)

        def one(h, carry):
            pt, ds = score_grads(p, h)
            acc_k[:, lanes(h)] += nn(ds, q[rows, lanes(h)])
            acc_v[:, lanes(h)] += nn(pt.astype(BF), ga_s[:, lanes(h)])
            g[rows, lanes(h)] = nn(kt[h], ds).T.astype(BF)
            return carry

        lax.fori_loop(0, HEADS_HERE, one, 0)


    def grad_attn_first():
        for p in (0, 1):
            ga_f[pl.ds(p * PAIR, PAIR)] = nt(cot[pl.ds(p * PAIR, PAIR)], wo[...]).astype(BF)

    def backward_first(h):
        rows = pl.ds(0, 2 * PAIR)
        dp = nt(kv[:, v_lanes(h)], ga_f[:, lanes(h)])
        for p in (0, 1):
            pt = probs[p * HEADS_HERE + h]
            dpp = dp[:, p * PAIR : (p + 1) * PAIR]
            delta = jnp.sum(pt * dpp, axis=0, keepdims=True)
            ds_f[:, pl.ds(p * PAIR, PAIR)] = (pt * (dpp - delta) * SCALE).astype(BF)
            pb_f[:, pl.ds(p * PAIR, PAIR)] = pt.astype(BF)
        acc_k[:, lanes(h)] = nn(ds_f[...], q[rows, lanes(h)])
        acc_v[:, lanes(h)] = nn(pb_f[...], ga_f[:, lanes(h)])
        g[rows, lanes(h)] = nn(kt[h], ds_f[...]).T.astype(BF)

    forward(1, 1, 0)
    forward(1, 1, 1)
    got(1, 1, (1, 3))
    got(1, 2, (0, 2))
    got(1, 3)
    grad_attn_first()
    backward_first(0)
    spread(1, 3)
    backward_first(1)
    forward(1, 1, 2)
    backward_first(2)
    forward(1, 1, 3)
    got(1, 5, (1, 3))
    backward(2)
    got(1, 6, (0, 2))
    got(1, 7)

    last = pl.ds(3 * PAIR, PAIR)
    own = pl.ds(0, FRAME)
    prev = pl.ds(FRAME, FRAME)
    ga_s[...] = nt(cot[last], wo[...]).astype(BF)

    def last_prev(h, carry):
        pt, ds = score_grads(3, h)
        ds_s[h] = ds
        back_s[:, lanes(h)] = (acc_k[prev, lanes(h)] + nn(ds[FRAME:], q[last, lanes(h)])).astype(BF)
        back_s[:, v_lanes(h)] = (acc_v[prev, lanes(h)] + nn(pt[FRAME:].astype(BF), ga_s[:, lanes(h)])).astype(BF)
        return carry

    lax.fori_loop(0, HEADS_HERE, last_prev, 0)
    pieces = ((448, 64), (256, 192), (0, 256))
    backs = []
    for i, (start, size) in enumerate(pieces):
        rows = pl.ds(start, size)
        backs.append(push(back_s.at[rows], back_r.at[rows], bs_sem.at[i], br_sem.at[i], before))

    def last_own(h, carry):
        g[last, lanes(h)] = nn(kt[h], ds_s[h]).T.astype(BF)
        acc_k[own, lanes(h)] += nn(ds_s[h, own], q[last, lanes(h)])
        acc_v[own, lanes(h)] += nn(probs[3 * HEADS_HERE + h, own].astype(BF), ga_s[:, lanes(h)])
        return carry

    lax.fori_loop(0, HEADS_HERE, last_own, 0)

    def join(i):
        rows = pl.ds(*pieces[i])
        backs[i].wait_recv()
        g[rows, pl.ds(WIDTH, WIDTH)] = (acc_k[rows] + back_r[rows, pl.ds(0, WIDTH)].astype(F32)).astype(BF)
        g[rows, pl.ds(2 * WIDTH, WIDTH)] = (acc_v[rows] + back_r[rows, pl.ds(WIDTH, WIDTH)].astype(F32)).astype(BF)

    def partials(i, hf):
        rows = pl.ds(*pieces[i])

        def tile(n, carry):
            w_rows = pl.ds(pl.multiple_of(hf * COLS + n * 384, 128), 384)
            total = nt(g[rows, pl.ds(0, WIDTH)], wq[0, w_rows])
            total += nt(g[rows, pl.ds(WIDTH, WIDTH)], wq[1, w_rows])
            total += nt(g[rows, pl.ds(2 * WIDTH, WIDTH)], wq[2, w_rows])
            part[hf, rows, pl.ds(pl.multiple_of(n * 384, 128), 384)] = total.astype(BF)
            return carry

        lax.fori_loop(0, COLS // 384, tile, 0)

    sums = {}

    def sum_push(key, i, src, dst, peer):
        zz, hf = key
        k = (zz * PARTS + hf) * 6 + i
        sums[key, i] = push(src, dst, rs_sem.at[k], rr_sem.at[k], peer)

    def opposite(zz, hf):
        u = zz * PARTS + hf
        sum_push((zz, hf), 0, part.at[hf, chunk(4 * zz + 3, 0)], ra.at[u], right)
        sum_push((zz, hf), 1, part.at[hf, chunk(4 * zz + 3, 1)], rb.at[u], left)

    def singles(zz, hf):
        u = zz * PARTS + hf
        sum_push((zz, hf), 2, part.at[hf, chunk(4 * zz + 2, 1)], rl.at[u, pl.ds(HALF, HALF)], right)
        sum_push((zz, hf), 3, part.at[hf, chunk(4 * zz + 1, 0)], rr.at[u, pl.ds(0, HALF)], left)

    def doubles(zz, hf):
        u = zz * PARTS + hf
        for_right = chunk(4 * zz + 2, 0)
        for_left = chunk(4 * zz + 1, 1)
        sums[(zz, hf), 0].wait_recv()
        part[hf, for_right] = (part[hf, for_right].astype(F32) + ra[u].astype(F32)).astype(BF)
        sum_push((zz, hf), 4, part.at[hf, for_right], rl.at[u, pl.ds(0, HALF)], right)
        sums[(zz, hf), 1].wait_recv()
        part[hf, for_left] = (part[hf, for_left].astype(F32) + rb[u].astype(F32)).astype(BF)
        sum_push((zz, hf), 5, part.at[hf, for_left], rr.at[u, pl.ds(HALF, HALF)], left)

    crossing = {}

    def cross(hf):
        for i in (2, 3, 4, 5):
            sums[(1, hf), i].wait_recv()
        mine = part[hf, pl.ds(256, BLOCK)].astype(F32)
        zs[hf] = (mine + rl[PARTS + hf].astype(F32) + rr[PARTS + hf].astype(F32)).astype(BF)
        crossing[hf] = push(zs.at[hf], rz.at[hf], zs_sem.at[hf], zr_sem.at[hf], across)

    join(0)
    for hf in range(PARTS):
        partials(0, hf)
        opposite(1, hf)
    join(1)
    for hf in range(PARTS):
        partials(1, hf)
        singles(1, hf)
        doubles(1, hf)
    join(2)
    for hf in range(PARTS):
        partials(2, hf)
        opposite(0, hf)
        singles(0, hf)
        cross(hf)
    for hf in range(PARTS):
        doubles(0, hf)
    own_rows = pl.ds(0, BLOCK)
    scale = inv[:, pl.ds(0, 1)]
    inner = jnp.zeros((BLOCK, 1), F32)
    for hf in range(PARTS):
        cols = pl.ds(hf * COLS, COLS)
        for i in (2, 3, 4, 5):
            sums[(0, hf), i].wait_recv()
        crossing[hf].wait_recv()
        total = part[hf, own_rows].astype(F32) + rl[hf].astype(F32) + rr[hf].astype(F32) + rz[hf].astype(F32)
        total = total * gain[:, cols]
        inner += jnp.sum(total * (lat[:, cols].astype(F32) * scale), axis=-1, keepdims=True)
        grad[:, cols] = total
    inner = inner * (1.0 / D)
    for hf in range(PARTS):
        cols = pl.ds(hf * COLS, COLS)
        normed = lat[:, cols].astype(F32) * scale
        out_ref[:, cols] = (cot[own_rows, cols].astype(F32) + scale * (grad[:, cols] - normed * inner)).astype(BF)

    for copy in sent:
        copy.wait_send()


def shards(latents, cotangent, norm_gain, w_qkv, w_out):
    hbm = pl.BlockSpec(memory_space=pl.ANY)
    dma = pltpu.SemaphoreType.DMA
    return pl.pallas_call(
        kernel,
        out_shape=jax.ShapeDtypeStruct((BLOCK, D), BF),
        in_specs=[hbm] * 5,
        out_specs=pl.BlockSpec(memory_space=pltpu.VMEM),
        scratch_shapes=[
            pltpu.VMEM((BLOCK, D), BF),
            pltpu.VMEM((1, D), F32),
            pltpu.VMEM((3, D, WIDTH), BF),
            pltpu.VMEM((WIDTH, D), BF),
            pltpu.VMEM((FRAME, D), BF),
            pltpu.VMEM((FRAME, D), BF),
            pltpu.VMEM((BLOCK, 128), F32),
            pltpu.VMEM((FRAME, WIDTH), BF),
            pltpu.VMEM((2 * FRAME, 2 * WIDTH), BF),
            pltpu.VMEM((HEADS_HERE, HEAD_DIM, 2 * FRAME), BF),
            pltpu.VMEM((4 * HEADS_HERE, 2 * FRAME, PAIR), F32),
            pltpu.VMEM((2 * FRAME, WIDTH), F32),
            pltpu.VMEM((2 * FRAME, WIDTH), F32),
            pltpu.VMEM((FRAME, 2 * WIDTH), BF),
            pltpu.VMEM((FRAME, 2 * WIDTH), BF),
            pltpu.VMEM((FRAME, 3 * WIDTH), BF),
            pltpu.VMEM((PARTS, FRAME, COLS), BF),
            pltpu.VMEM((2 * PARTS, HALF, COLS), BF),
            pltpu.VMEM((2 * PARTS, HALF, COLS), BF),
            pltpu.VMEM((2 * PARTS, BLOCK, COLS), BF),
            pltpu.VMEM((2 * PARTS, BLOCK, COLS), BF),
            pltpu.VMEM((PARTS, BLOCK, COLS), BF),
            pltpu.VMEM((PARTS, BLOCK, COLS), BF),
            pltpu.VMEM((PAIR, WIDTH), BF),
            pltpu.VMEM((HEADS_HERE, 2 * FRAME, PAIR), BF),
            pltpu.VMEM((2 * PAIR, WIDTH), BF),
            pltpu.VMEM((2 * FRAME, 2 * PAIR), BF),
            pltpu.VMEM((2 * FRAME, 2 * PAIR), BF),
            pltpu.VMEM((BLOCK, D), F32),
            dma((5,)),
            dma((2, 32)),
            dma((2, 32)),
            dma((4,)),
            dma((4,)),
            dma((3,)),
            dma((3,)),
            dma((12 * PARTS,)),
            dma((12 * PARTS,)),
            dma((PARTS,)),
            dma((PARTS,)),
        ],
        compiler_params=pltpu.CompilerParams(
            collective_id=0, has_side_effects=True, vmem_limit_bytes=56 * 1024 * 1024
        ),
        name="frame_attention_grad",
    )(latents, cotangent, norm_gain.reshape(1, D), jnp.transpose(w_qkv, (1, 0, 2)), w_out)


def solution(mesh):
    return jax.shard_map(
        shards,
        mesh=mesh,
        in_specs=(
            P(("tm", "head"), None),
            P(("tm", "head"), None),
            P(),
            P(None, None, "head"),
            P("head", None),
        ),
        out_specs=P(("tm", "head"), None),
        check_vma=False,
    )
```

```python
import functools

import jax
import jax.numpy as jnp
from jax import lax
from jax.experimental import pallas as pl
from jax.experimental.pallas import tpu as pltpu
from jax.sharding import PartitionSpec as P

EPSILON = 1e-06
MESH = pl.DeviceIdType.MESH
D = 3072
HEAD_DIM = 128
HEADS_HERE = 3
WIDTH = HEADS_HERE * HEAD_DIM
BLOCK = 64
HALF = BLOCK // 2
STEP = BLOCK // 4
FRAME = 512
PAIR = 2 * BLOCK
PARTS = 4
COLS = D // PARTS
N_TM = 32
X = 4
SCALE = HEAD_DIM ** (-0.5)
BF = jnp.bfloat16
F32 = jnp.float32


def nt(a, b):
    return lax.dot_general(a, b, (((1,), (1,)), ((), ())), preferred_element_type=F32)


def nn(a, b):
    return jnp.dot(a, b, preferred_element_type=F32)


def kernel(
    lat_h, cot_h, gain_h, wqkv_h, wout_h, out_ref,
    lat, gain, wq, wo, hid, cot, inv, q, kv, kt, probs, acc_k, acc_v, back_s, back_r, g,
    part, ra, rb, rl, rr, zs, rz, ga_s, ds_s, ga_f, ds_f, pb_f, grad,
    ld_sem, gs_sem, gr_sem, kvs_sem, kvr_sem, bs_sem, br_sem, rs_sem, rr_sem, zs_sem, zr_sem,
):
    tm = lax.axis_index("tm")
    head = lax.axis_index("head")
    x = lax.rem(head, X)
    base = head - x
    right = (tm, base + lax.rem(x + 1, X))
    left = (tm, base + lax.rem(x + X - 1, X))
    across = (tm, lax.rem(head + X, 2 * X))
    after = (lax.rem(tm + 1, N_TM), head)
    before = (lax.rem(tm + N_TM - 1, N_TM), head)

    barrier = pltpu.get_barrier_semaphore()
    for peer in (right, left, across, after, before):
        pl.semaphore_signal(barrier, inc=1, device_id=peer, device_id_type=MESH)

    loads = [
        pltpu.make_async_copy(lat_h, lat, ld_sem.at[0]),
        pltpu.make_async_copy(gain_h, gain, ld_sem.at[1]),
        pltpu.make_async_copy(cot_h, cot.at[pl.ds(0, BLOCK)], ld_sem.at[2]),
        pltpu.make_async_copy(wqkv_h, wq, ld_sem.at[3]),
        pltpu.make_async_copy(wout_h, wo, ld_sem.at[4]),
    ]
    for load in loads:
        load.start()
    loads[0].wait()
    loads[1].wait()
    for r in range(4):
        rows = pl.ds(r * 16, 16)
        lf = lat[rows].astype(F32)
        scale = lax.rsqrt(jnp.mean(lf * lf, axis=-1, keepdims=True) + EPSILON)
        inv[rows] = jnp.broadcast_to(scale, (16, 128))
        hid[rows] = (lf * scale * gain[...]).astype(BF)
    pl.semaphore_wait(barrier, 5)

    sent = []

    def push(src, dst, s_sem, r_sem, peer):
        copy = pltpu.make_async_remote_copy(
            src_ref=src, dst_ref=dst, send_sem=s_sem, recv_sem=r_sem, device_id=peer, device_id_type=MESH
        )
        copy.start()
        sent.append(copy)
        return copy

    def chunk(slot, c):
        return pl.ds(slot * BLOCK + c * HALF, HALF)

    bufs = (hid, cot)
    moves = {}

    def gather_push(a, src_slot, dst_slot, c, peer):
        i = dst_slot * 4 + c
        moves[a, dst_slot, c] = push(
            bufs[a].at[pl.ds(src_slot * BLOCK + c * STEP, STEP)], bufs[a].at[pl.ds(dst_slot * BLOCK + c * STEP, STEP)],
            gs_sem.at[a, i], gr_sem.at[a, i], peer,
        )

    def got(a, slot, cs=(0, 1, 2, 3)):
        for c in cs:
            moves[a, slot, c].wait_recv()

    def to_right(a, zz, c):
        gather_push(a, 4 * zz, 4 * zz + 1, c, right)

    def to_left(a, zz, c):
        gather_push(a, 4 * zz, 4 * zz + 2, c, left)

    def spread(a, c):
        got(a, 4, (c,))
        to_right(a, 1, c)
        to_left(a, 1, c)

    def forward(a, zz, c):
        near = 4 * zz + 1 + c % 2
        got(a, near, (c,))
        gather_push(a, near, 4 * zz + 3, c, left if c % 2 else right)

    kv_copies = []

    def project(p):
        rows = pl.ds(p * PAIR, PAIR)
        h = hid[rows]
        q[rows] = nn(h, wq[0]).astype(BF)
        kv[rows, pl.ds(0, WIDTH)] = nn(h, wq[1]).astype(BF)
        kv[rows, pl.ds(WIDTH, WIDTH)] = nn(h, wq[2]).astype(BF)
        kv_copies.append(
            push(kv.at[rows], kv.at[pl.ds(FRAME + p * PAIR, PAIR)], kvs_sem.at[p], kvr_sem.at[p], after)
        )

    for c in range(4):
        gather_push(0, 0, 4, c, across)
        to_right(0, 0, (0, 2, 1, 3)[c])
        to_left(0, 0, (1, 3, 0, 2)[c])
    loads[2].wait()
    for c in range(4):
        forward(0, 0, c)
        (to_left if c % 2 else to_right)(1, 0, c)
    loads[3].wait()
    got(0, 1, (1, 3))
    project(0)
    spread(0, 0)
    spread(0, 1)
    for c in range(4):
        (to_right if c % 2 else to_left)(1, 0, c)
    got(0, 2, (0, 2))
    got(0, 3)
    project(1)
    spread(0, 2)
    for c in range(4):
        gather_push(1, 0, 4, c, across)
    spread(0, 3)
    for c in range(4):
        forward(0, 1, c)
    for c in range(4):
        forward(1, 0, c)
    got(0, 5, (1, 3))
    project(2)
    spread(1, 0)
    got(0, 6, (0, 2))
    got(0, 7)
    project(3)
    spread(1, 1)
    loads[4].wait()

    def lanes(h):
        if isinstance(h, int):
            return pl.ds(h * HEAD_DIM, HEAD_DIM)
        return pl.ds(pl.multiple_of(h * HEAD_DIM, HEAD_DIM), HEAD_DIM)

    def v_lanes(h):
        if isinstance(h, int):
            return pl.ds(WIDTH + h * HEAD_DIM, HEAD_DIM)
        return pl.ds(pl.multiple_of(WIDTH + h * HEAD_DIM, HEAD_DIM), HEAD_DIM)

    def turn(rows):
        def one(h, carry):
            kt[h, :, rows] = kv[rows, lanes(h)].astype(F32).T.astype(BF)
            return carry

        lax.fori_loop(0, HEADS_HERE, one, 0)

    own = pl.ds(0, FRAME)
    prev = pl.ds(FRAME, FRAME)

    def queries_of(i):
        p = i // HEADS_HERE
        h = i - p * HEADS_HERE
        return h, q[pl.ds(pl.multiple_of(p * PAIR, PAIR), PAIR), lanes(h)]

    def score_own(i, carry):
        h, qh = queries_of(i)
        probs[i, own] = nt(kv[own, lanes(h)], qh) * SCALE
        return carry

    def score(i, carry):
        h, qh = queries_of(i)
        own_s = probs[i, own]
        prev_s = jnp.where(tm > 0, nt(kv[prev, lanes(h)], qh) * SCALE, -1e30)
        top = jnp.maximum(jnp.max(own_s, axis=0, keepdims=True), jnp.max(prev_s, axis=0, keepdims=True))
        own_e = jnp.exp(own_s - top)
        prev_e = jnp.exp(prev_s - top)
        part_of = 1.0 / (jnp.sum(own_e, axis=0, keepdims=True) + jnp.sum(prev_e, axis=0, keepdims=True))
        probs[i, own] = own_e * part_of
        probs[i, prev] = prev_e * part_of
        return carry

    lax.fori_loop(0, 4 * HEADS_HERE, score_own, 0)
    turn(own)
    got(1, 1, (1, 3))
    got(1, 2, (0, 2))
    got(1, 3)
    for p in (0, 1):
        ga_f[pl.ds(p * PAIR, PAIR)] = nt(cot[pl.ds(p * PAIR, PAIR)], wo[...]).astype(BF)
    for copy in kv_copies:
        copy.wait_recv()
    turn(prev)

    lax.fori_loop(0, 2 * HEADS_HERE, score, 0)
    spread(1, 2)
    lax.fori_loop(2 * HEADS_HERE, 4 * HEADS_HERE, score, 0)

    def score_grads(p, h):
        pt = probs[p * HEADS_HERE + h]
        dp = nt(kv[:, v_lanes(h)], ga_s[:, lanes(h)])
        delta = jnp.sum(pt * dp, axis=0, keepdims=True)
        return pt, (pt * (dp - delta) * SCALE).astype(BF)

    def backward(p):
        rows = pl.ds(p * PAIR, PAIR)
        ga_s[...] = nt(cot[rows], wo[...]).astype(BF)

        def one(h, carry):
            pt, ds = score_grads(p, h)
            acc_k[:, lanes(h)] += nn(ds, q[rows, lanes(h)])
            acc_v[:, lanes(h)] += nn(pt.astype(BF), ga_s[:, lanes(h)])
            g[rows, lanes(h)] = nn(kt[h], ds).T.astype(BF)
            return carry

        lax.fori_loop(0, HEADS_HERE, one, 0)


    def backward_first(h):
        rows = pl.ds(0, 2 * PAIR)
        dp = nt(kv[:, v_lanes(h)], ga_f[:, lanes(h)])
        for p in (0, 1):
            pt = probs[p * HEADS_HERE + h]
            dpp = dp[:, p * PAIR : (p + 1) * PAIR]
            delta = jnp.sum(pt * dpp, axis=0, keepdims=True)
            ds_f[:, pl.ds(p * PAIR, PAIR)] = (pt * (dpp - delta) * SCALE).astype(BF)
            pb_f[:, pl.ds(p * PAIR, PAIR)] = pt.astype(BF)
        acc_k[:, lanes(h)] = nn(ds_f[...], q[rows, lanes(h)])
        acc_v[:, lanes(h)] = nn(pb_f[...], ga_f[:, lanes(h)])
        g[rows, lanes(h)] = nn(kt[h], ds_f[...]).T.astype(BF)

    forward(1, 1, 0)
    forward(1, 1, 1)
    backward_first(0)
    spread(1, 3)
    backward_first(1)
    forward(1, 1, 2)
    backward_first(2)
    forward(1, 1, 3)
    got(1, 5, (1, 3))
    backward(2)
    got(1, 6, (0, 2))
    got(1, 7)

    last = pl.ds(3 * PAIR, PAIR)
    ga_s[...] = nt(cot[last], wo[...]).astype(BF)

    def last_prev(h, carry):
        pt, ds = score_grads(3, h)
        ds_s[h] = ds
        back_s[:, lanes(h)] = (acc_k[prev, lanes(h)] + nn(ds[FRAME:], q[last, lanes(h)])).astype(BF)
        back_s[:, v_lanes(h)] = (acc_v[prev, lanes(h)] + nn(pt[FRAME:].astype(BF), ga_s[:, lanes(h)])).astype(BF)
        return carry

    lax.fori_loop(0, HEADS_HERE, last_prev, 0)
    pieces = ((448, 64), (256, 192), (0, 256))
    backs = []
    for i, (start, size) in enumerate(pieces):
        rows = pl.ds(start, size)
        backs.append(push(back_s.at[rows], back_r.at[rows], bs_sem.at[i], br_sem.at[i], before))

    def last_own(h, carry):
        g[last, lanes(h)] = nn(kt[h], ds_s[h]).T.astype(BF)
        acc_k[own, lanes(h)] += nn(ds_s[h, own], q[last, lanes(h)])
        acc_v[own, lanes(h)] += nn(probs[3 * HEADS_HERE + h, own].astype(BF), ga_s[:, lanes(h)])
        return carry

    lax.fori_loop(0, HEADS_HERE, last_own, 0)

    def join(i):
        rows = pl.ds(*pieces[i])
        backs[i].wait_recv()
        g[rows, pl.ds(WIDTH, WIDTH)] = (acc_k[rows] + back_r[rows, pl.ds(0, WIDTH)].astype(F32)).astype(BF)
        g[rows, pl.ds(2 * WIDTH, WIDTH)] = (acc_v[rows] + back_r[rows, pl.ds(WIDTH, WIDTH)].astype(F32)).astype(BF)

    def partials(i, hf):
        rows = pl.ds(*pieces[i])

        def tile(n, carry):
            w_rows = pl.ds(pl.multiple_of(hf * COLS + n * 384, 128), 384)
            total = nt(g[rows, pl.ds(0, WIDTH)], wq[0, w_rows])
            total += nt(g[rows, pl.ds(WIDTH, WIDTH)], wq[1, w_rows])
            total += nt(g[rows, pl.ds(2 * WIDTH, WIDTH)], wq[2, w_rows])
            part[hf, rows, pl.ds(pl.multiple_of(n * 384, 128), 384)] = total.astype(BF)
            return carry

        lax.fori_loop(0, COLS // 384, tile, 0)

    sums = {}

    def sum_push(key, i, src, dst, peer):
        zz, hf = key
        k = (zz * PARTS + hf) * 6 + i
        sums[key, i] = push(src, dst, rs_sem.at[k], rr_sem.at[k], peer)

    def opposite(zz, hf):
        u = zz * PARTS + hf
        sum_push((zz, hf), 0, part.at[hf, chunk(4 * zz + 3, 0)], ra.at[u], right)
        sum_push((zz, hf), 1, part.at[hf, chunk(4 * zz + 3, 1)], rb.at[u], left)

    def singles(zz, hf):
        u = zz * PARTS + hf
        sum_push((zz, hf), 2, part.at[hf, chunk(4 * zz + 2, 1)], rl.at[u, pl.ds(HALF, HALF)], right)
        sum_push((zz, hf), 3, part.at[hf, chunk(4 * zz + 1, 0)], rr.at[u, pl.ds(0, HALF)], left)

    def doubles(zz, hf):
        u = zz * PARTS + hf
        for_right = chunk(4 * zz + 2, 0)
        for_left = chunk(4 * zz + 1, 1)
        sums[(zz, hf), 0].wait_recv()
        part[hf, for_right] = (part[hf, for_right].astype(F32) + ra[u].astype(F32)).astype(BF)
        sum_push((zz, hf), 4, part.at[hf, for_right], rl.at[u, pl.ds(0, HALF)], right)
        sums[(zz, hf), 1].wait_recv()
        part[hf, for_left] = (part[hf, for_left].astype(F32) + rb[u].astype(F32)).astype(BF)
        sum_push((zz, hf), 5, part.at[hf, for_left], rr.at[u, pl.ds(HALF, HALF)], left)

    crossing = {}

    def cross(hf):
        for i in (2, 3, 4, 5):
            sums[(1, hf), i].wait_recv()
        mine = part[hf, pl.ds(256, BLOCK)].astype(F32)
        zs[hf] = (mine + rl[PARTS + hf].astype(F32) + rr[PARTS + hf].astype(F32)).astype(BF)
        crossing[hf] = push(zs.at[hf], rz.at[hf], zs_sem.at[hf], zr_sem.at[hf], across)

    join(0)
    for hf in range(PARTS):
        partials(0, hf)
        opposite(1, hf)
    join(1)
    for hf in range(PARTS):
        partials(1, hf)
        singles(1, hf)
        doubles(1, hf)
    join(2)
    for hf in range(PARTS):
        partials(2, hf)
        opposite(0, hf)
        singles(0, hf)
        cross(hf)
    for hf in range(PARTS):
        doubles(0, hf)
    own_rows = pl.ds(0, BLOCK)
    scale = inv[:, pl.ds(0, 1)]
    inner = jnp.zeros((BLOCK, 1), F32)
    for hf in range(PARTS):
        cols = pl.ds(hf * COLS, COLS)
        for i in (2, 3, 4, 5):
            sums[(0, hf), i].wait_recv()
        crossing[hf].wait_recv()
        total = part[hf, own_rows].astype(F32) + rl[hf].astype(F32) + rr[hf].astype(F32) + rz[hf].astype(F32)
        total = total * gain[:, cols]
        inner += jnp.sum(total * (lat[:, cols].astype(F32) * scale), axis=-1, keepdims=True)
        grad[:, cols] = total
    inner = inner * (1.0 / D)
    for hf in range(PARTS):
        cols = pl.ds(hf * COLS, COLS)
        normed = lat[:, cols].astype(F32) * scale
        out_ref[:, cols] = (cot[own_rows, cols].astype(F32) + scale * (grad[:, cols] - normed * inner)).astype(BF)

    for copy in sent:
        copy.wait_send()


def shards(latents, cotangent, norm_gain, w_qkv, w_out):
    hbm = pl.BlockSpec(memory_space=pl.ANY)
    dma = pltpu.SemaphoreType.DMA
    return pl.pallas_call(
        kernel,
        out_shape=jax.ShapeDtypeStruct((BLOCK, D), BF),
        in_specs=[hbm] * 5,
        out_specs=pl.BlockSpec(memory_space=pltpu.VMEM),
        scratch_shapes=[
            pltpu.VMEM((BLOCK, D), BF),
            pltpu.VMEM((1, D), F32),
            pltpu.VMEM((3, D, WIDTH), BF),
            pltpu.VMEM((WIDTH, D), BF),
            pltpu.VMEM((FRAME, D), BF),
            pltpu.VMEM((FRAME, D), BF),
            pltpu.VMEM((BLOCK, 128), F32),
            pltpu.VMEM((FRAME, WIDTH), BF),
            pltpu.VMEM((2 * FRAME, 2 * WIDTH), BF),
            pltpu.VMEM((HEADS_HERE, HEAD_DIM, 2 * FRAME), BF),
            pltpu.VMEM((4 * HEADS_HERE, 2 * FRAME, PAIR), F32),
            pltpu.VMEM((2 * FRAME, WIDTH), F32),
            pltpu.VMEM((2 * FRAME, WIDTH), F32),
            pltpu.VMEM((FRAME, 2 * WIDTH), BF),
            pltpu.VMEM((FRAME, 2 * WIDTH), BF),
            pltpu.VMEM((FRAME, 3 * WIDTH), BF),
            pltpu.VMEM((PARTS, FRAME, COLS), BF),
            pltpu.VMEM((2 * PARTS, HALF, COLS), BF),
            pltpu.VMEM((2 * PARTS, HALF, COLS), BF),
            pltpu.VMEM((2 * PARTS, BLOCK, COLS), BF),
            pltpu.VMEM((2 * PARTS, BLOCK, COLS), BF),
            pltpu.VMEM((PARTS, BLOCK, COLS), BF),
            pltpu.VMEM((PARTS, BLOCK, COLS), BF),
            pltpu.VMEM((PAIR, WIDTH), BF),
            pltpu.VMEM((HEADS_HERE, 2 * FRAME, PAIR), BF),
            pltpu.VMEM((2 * PAIR, WIDTH), BF),
            pltpu.VMEM((2 * FRAME, 2 * PAIR), BF),
            pltpu.VMEM((2 * FRAME, 2 * PAIR), BF),
            pltpu.VMEM((BLOCK, D), F32),
            dma((5,)),
            dma((2, 32)),
            dma((2, 32)),
            dma((4,)),
            dma((4,)),
            dma((3,)),
            dma((3,)),
            dma((12 * PARTS,)),
            dma((12 * PARTS,)),
            dma((PARTS,)),
            dma((PARTS,)),
        ],
        compiler_params=pltpu.CompilerParams(
            collective_id=0, has_side_effects=True, vmem_limit_bytes=56 * 1024 * 1024
        ),
        name="frame_attention_grad",
    )(latents, cotangent, norm_gain.reshape(1, D), jnp.transpose(w_qkv, (1, 0, 2)), w_out)


def solution(mesh):
    return jax.shard_map(
        shards,
        mesh=mesh,
        in_specs=(
            P(("tm", "head"), None),
            P(("tm", "head"), None),
            P(),
            P(None, None, "head"),
            P("head", None),
        ),
        out_specs=P(("tm", "head"), None),
        check_vma=False,
    )
```

```python
import functools

import jax
import jax.numpy as jnp
from jax import lax
from jax.experimental import pallas as pl
from jax.experimental.pallas import tpu as pltpu
from jax.sharding import PartitionSpec as P

EPSILON = 1e-06
MESH = pl.DeviceIdType.MESH
D = 3072
HEAD_DIM = 128
HEADS_HERE = 3
WIDTH = HEADS_HERE * HEAD_DIM
BLOCK = 64
HALF = BLOCK // 2
STEP = BLOCK // 4
FRAME = 512
PAIR = 2 * BLOCK
PARTS = 4
COLS = D // PARTS
N_TM = 32
X = 4
SCALE = HEAD_DIM ** (-0.5)
BF = jnp.bfloat16
F32 = jnp.float32


def nt(a, b):
    return lax.dot_general(a, b, (((1,), (1,)), ((), ())), preferred_element_type=F32)


def nn(a, b):
    return jnp.dot(a, b, preferred_element_type=F32)


def kernel(
    lat_h, cot_h, gain_h, wqkv_h, wout_h, out_ref,
    lat, gain, wq, wo, hid, cot, inv, q, kv, kt, probs, acc_k, acc_v, back_s, back_r, g,
    part, ra, rb, rl, rr, zs, rz, ga_s, ds_s, ga_f, ds_f, pb_f, grad,
    ld_sem, gs_sem, gr_sem, kvs_sem, kvr_sem, bs_sem, br_sem, rs_sem, rr_sem, zs_sem, zr_sem, z_ready, tm_ready,
):
    tm = lax.axis_index("tm")
    head = lax.axis_index("head")
    x = lax.rem(head, X)
    base = head - x
    right = (tm, base + lax.rem(x + 1, X))
    left = (tm, base + lax.rem(x + X - 1, X))
    across = (tm, lax.rem(head + X, 2 * X))
    after = (lax.rem(tm + 1, N_TM), head)
    before = (lax.rem(tm + N_TM - 1, N_TM), head)

    barrier = pltpu.get_barrier_semaphore()
    for peer in (right, left, before):
        pl.semaphore_signal(barrier, inc=1, device_id=peer, device_id_type=MESH)

    @pl.when(head < X)
    def _():
        pl.semaphore_signal(barrier, inc=1, device_id=across, device_id_type=MESH)

    loads = [
        pltpu.make_async_copy(lat_h, lat, ld_sem.at[0]),
        pltpu.make_async_copy(gain_h, gain, ld_sem.at[1]),
        pltpu.make_async_copy(cot_h, cot.at[pl.ds(0, BLOCK)], ld_sem.at[2]),
        pltpu.make_async_copy(wqkv_h, wq, ld_sem.at[3]),
        pltpu.make_async_copy(wout_h, wo, ld_sem.at[4]),
    ]
    for load in loads:
        load.start()
    loads[0].wait()
    loads[1].wait()
    for r in range(4):
        rows = pl.ds(r * 16, 16)
        lf = lat[rows].astype(F32)
        scale = lax.rsqrt(jnp.mean(lf * lf, axis=-1, keepdims=True) + EPSILON)
        inv[rows] = jnp.broadcast_to(scale, (16, 128))
        hid[rows] = (lf * scale * gain[...]).astype(BF)
    @pl.when(head < X)
    def _():
        pl.semaphore_wait(barrier, 3)

    @pl.when(head >= X)
    def _():
        pl.semaphore_wait(barrier, 4)
        pl.semaphore_signal(z_ready, inc=1, device_id=across, device_id_type=MESH)

    pl.semaphore_signal(tm_ready, inc=1, device_id=after, device_id_type=MESH)

    sent = []

    def push(src, dst, s_sem, r_sem, peer):
        copy = pltpu.make_async_remote_copy(
            src_ref=src, dst_ref=dst, send_sem=s_sem, recv_sem=r_sem, device_id=peer, device_id_type=MESH
        )
        copy.start()
        sent.append(copy)
        return copy

    def chunk(slot, c):
        return pl.ds(slot * BLOCK + c * HALF, HALF)

    bufs = (hid, cot)
    moves = {}

    def gather_push(a, src_slot, dst_slot, c, peer):
        i = dst_slot * 4 + c
        moves[a, dst_slot, c] = push(
            bufs[a].at[pl.ds(src_slot * BLOCK + c * STEP, STEP)], bufs[a].at[pl.ds(dst_slot * BLOCK + c * STEP, STEP)],
            gs_sem.at[a, i], gr_sem.at[a, i], peer,
        )

    def got(a, slot, cs=(0, 1, 2, 3)):
        for c in cs:
            moves[a, slot, c].wait_recv()

    def to_right(a, zz, c):
        gather_push(a, 4 * zz, 4 * zz + 1, c, right)

    def to_left(a, zz, c):
        gather_push(a, 4 * zz, 4 * zz + 2, c, left)

    def spread(a, c):
        got(a, 4, (c,))
        to_right(a, 1, c)
        to_left(a, 1, c)

    def forward(a, zz, c):
        near = 4 * zz + 1 + c % 2
        got(a, near, (c,))
        gather_push(a, near, 4 * zz + 3, c, left if c % 2 else right)

    kv_copies = []

    def project(p):
        rows = pl.ds(p * PAIR, PAIR)
        h = hid[rows]
        q[rows] = nn(h, wq[0]).astype(BF)
        kv[rows, pl.ds(0, WIDTH)] = nn(h, wq[1]).astype(BF)
        kv[rows, pl.ds(WIDTH, WIDTH)] = nn(h, wq[2]).astype(BF)
        kv_copies.append(
            push(kv.at[rows], kv.at[pl.ds(FRAME + p * PAIR, PAIR)], kvs_sem.at[p], kvr_sem.at[p], after)
        )

    for c in range(4):
        to_right(0, 0, (0, 2, 1, 3)[c])
        to_left(0, 0, (1, 3, 0, 2)[c])

    @pl.when(head < X)
    def _():
        pl.semaphore_wait(z_ready, 1)

    for c in range(4):
        gather_push(0, 0, 4, c, across)
    loads[2].wait()
    for c in range(4):
        forward(0, 0, c)
        (to_left if c % 2 else to_right)(1, 0, c)
    loads[3].wait()
    got(0, 1, (1, 3))
    project(0)
    spread(0, 0)
    spread(0, 1)
    for c in range(4):
        (to_right if c % 2 else to_left)(1, 0, c)
    got(0, 2, (0, 2))
    got(0, 3)
    project(1)
    spread(0, 2)
    for c in range(4):
        gather_push(1, 0, 4, c, across)
    spread(0, 3)
    for c in range(4):
        forward(0, 1, c)
    for c in range(4):
        forward(1, 0, c)
    got(0, 5, (1, 3))
    project(2)
    spread(1, 0)
    got(0, 6, (0, 2))
    got(0, 7)
    project(3)
    spread(1, 1)
    loads[4].wait()

    def lanes(h):
        if isinstance(h, int):
            return pl.ds(h * HEAD_DIM, HEAD_DIM)
        return pl.ds(pl.multiple_of(h * HEAD_DIM, HEAD_DIM), HEAD_DIM)

    def v_lanes(h):
        if isinstance(h, int):
            return pl.ds(WIDTH + h * HEAD_DIM, HEAD_DIM)
        return pl.ds(pl.multiple_of(WIDTH + h * HEAD_DIM, HEAD_DIM), HEAD_DIM)

    def turn(rows):
        def one(h, carry):
            kt[h, :, rows] = kv[rows, lanes(h)].astype(F32).T.astype(BF)
            return carry

        lax.fori_loop(0, HEADS_HERE, one, 0)

    own = pl.ds(0, FRAME)
    prev = pl.ds(FRAME, FRAME)

    def queries_of(i):
        p = i // HEADS_HERE
        h = i - p * HEADS_HERE
        return h, q[pl.ds(pl.multiple_of(p * PAIR, PAIR), PAIR), lanes(h)]

    def score_own(i, carry):
        h, qh = queries_of(i)
        probs[i, own] = nt(kv[own, lanes(h)], qh) * SCALE
        return carry

    def score(i, carry):
        h, qh = queries_of(i)
        own_s = probs[i, own]
        prev_s = jnp.where(tm > 0, nt(kv[prev, lanes(h)], qh) * SCALE, -1e30)
        top = jnp.maximum(jnp.max(own_s, axis=0, keepdims=True), jnp.max(prev_s, axis=0, keepdims=True))
        own_e = jnp.exp(own_s - top)
        prev_e = jnp.exp(prev_s - top)
        part_of = 1.0 / (jnp.sum(own_e, axis=0, keepdims=True) + jnp.sum(prev_e, axis=0, keepdims=True))
        probs[i, own] = own_e * part_of
        probs[i, prev] = prev_e * part_of
        return carry

    lax.fori_loop(0, 4 * HEADS_HERE, score_own, 0)
    turn(own)
    got(1, 1, (1, 3))
    got(1, 2, (0, 2))
    got(1, 3)
    for p in (0, 1):
        ga_f[pl.ds(p * PAIR, PAIR)] = nt(cot[pl.ds(p * PAIR, PAIR)], wo[...]).astype(BF)
    for copy in kv_copies:
        copy.wait_recv()
    turn(prev)

    lax.fori_loop(0, 2 * HEADS_HERE, score, 0)
    spread(1, 2)
    lax.fori_loop(2 * HEADS_HERE, 4 * HEADS_HERE, score, 0)

    def score_grads(p, h):
        pt = probs[p * HEADS_HERE + h]
        dp = nt(kv[:, v_lanes(h)], ga_s[:, lanes(h)])
        delta = jnp.sum(pt * dp, axis=0, keepdims=True)
        return pt, (pt * (dp - delta) * SCALE).astype(BF)

    def backward(p):
        rows = pl.ds(p * PAIR, PAIR)
        ga_s[...] = nt(cot[rows], wo[...]).astype(BF)

        def one(h, carry):
            pt, ds = score_grads(p, h)
            acc_k[:, lanes(h)] += nn(ds, q[rows, lanes(h)])
            acc_v[:, lanes(h)] += nn(pt.astype(BF), ga_s[:, lanes(h)])
            g[rows, lanes(h)] = nn(kt[h], ds).T.astype(BF)
            return carry

        lax.fori_loop(0, HEADS_HERE, one, 0)


    def backward_first(h):
        rows = pl.ds(0, 2 * PAIR)
        dp = nt(kv[:, v_lanes(h)], ga_f[:, lanes(h)])
        for p in (0, 1):
            pt = probs[p * HEADS_HERE + h]
            dpp = dp[:, p * PAIR : (p + 1) * PAIR]
            delta = jnp.sum(pt * dpp, axis=0, keepdims=True)
            ds_f[:, pl.ds(p * PAIR, PAIR)] = (pt * (dpp - delta) * SCALE).astype(BF)
            pb_f[:, pl.ds(p * PAIR, PAIR)] = pt.astype(BF)
        acc_k[:, lanes(h)] = nn(ds_f[...], q[rows, lanes(h)])
        acc_v[:, lanes(h)] = nn(pb_f[...], ga_f[:, lanes(h)])
        g[rows, lanes(h)] = nn(kt[h], ds_f[...]).T.astype(BF)

    forward(1, 1, 0)
    forward(1, 1, 1)
    backward_first(0)
    spread(1, 3)
    backward_first(1)
    forward(1, 1, 2)
    backward_first(2)
    forward(1, 1, 3)
    got(1, 5, (1, 3))
    backward(2)
    got(1, 6, (0, 2))
    got(1, 7)

    last = pl.ds(3 * PAIR, PAIR)
    ga_s[...] = nt(cot[last], wo[...]).astype(BF)

    def last_prev(h, carry):
        pt, ds = score_grads(3, h)
        ds_s[h] = ds
        back_s[:, lanes(h)] = (acc_k[prev, lanes(h)] + nn(ds[FRAME:], q[last, lanes(h)])).astype(BF)
        back_s[:, v_lanes(h)] = (acc_v[prev, lanes(h)] + nn(pt[FRAME:].astype(BF), ga_s[:, lanes(h)])).astype(BF)
        return carry

    lax.fori_loop(0, HEADS_HERE, last_prev, 0)
    pieces = ((448, 64), (256, 192), (0, 256))
    pl.semaphore_wait(tm_ready, 1)
    backs = []
    for i, (start, size) in enumerate(pieces):
        rows = pl.ds(start, size)
        backs.append(push(back_s.at[rows], back_r.at[rows], bs_sem.at[i], br_sem.at[i], before))

    def last_own(h, carry):
        g[last, lanes(h)] = nn(kt[h], ds_s[h]).T.astype(BF)
        acc_k[own, lanes(h)] += nn(ds_s[h, own], q[last, lanes(h)])
        acc_v[own, lanes(h)] += nn(probs[3 * HEADS_HERE + h, own].astype(BF), ga_s[:, lanes(h)])
        return carry

    lax.fori_loop(0, HEADS_HERE, last_own, 0)

    def join(i):
        rows = pl.ds(*pieces[i])
        backs[i].wait_recv()
        g[rows, pl.ds(WIDTH, WIDTH)] = (acc_k[rows] + back_r[rows, pl.ds(0, WIDTH)].astype(F32)).astype(BF)
        g[rows, pl.ds(2 * WIDTH, WIDTH)] = (acc_v[rows] + back_r[rows, pl.ds(WIDTH, WIDTH)].astype(F32)).astype(BF)

    def partials(i, hf):
        rows = pl.ds(*pieces[i])

        def tile(n, carry):
            w_rows = pl.ds(pl.multiple_of(hf * COLS + n * 384, 128), 384)
            total = nt(g[rows, pl.ds(0, WIDTH)], wq[0, w_rows])
            total += nt(g[rows, pl.ds(WIDTH, WIDTH)], wq[1, w_rows])
            total += nt(g[rows, pl.ds(2 * WIDTH, WIDTH)], wq[2, w_rows])
            part[hf, rows, pl.ds(pl.multiple_of(n * 384, 128), 384)] = total.astype(BF)
            return carry

        lax.fori_loop(0, COLS // 384, tile, 0)

    sums = {}

    def sum_push(key, i, src, dst, peer):
        zz, hf = key
        k = (zz * PARTS + hf) * 6 + i
        sums[key, i] = push(src, dst, rs_sem.at[k], rr_sem.at[k], peer)

    def opposite(zz, hf):
        u = zz * PARTS + hf
        sum_push((zz, hf), 0, part.at[hf, chunk(4 * zz + 3, 0)], ra.at[u], right)
        sum_push((zz, hf), 1, part.at[hf, chunk(4 * zz + 3, 1)], rb.at[u], left)

    def singles(zz, hf):
        u = zz * PARTS + hf
        sum_push((zz, hf), 2, part.at[hf, chunk(4 * zz + 2, 1)], rl.at[u, pl.ds(HALF, HALF)], right)
        sum_push((zz, hf), 3, part.at[hf, chunk(4 * zz + 1, 0)], rr.at[u, pl.ds(0, HALF)], left)

    def doubles(zz, hf):
        u = zz * PARTS + hf
        for_right = chunk(4 * zz + 2, 0)
        for_left = chunk(4 * zz + 1, 1)
        sums[(zz, hf), 0].wait_recv()
        part[hf, for_right] = (part[hf, for_right].astype(F32) + ra[u].astype(F32)).astype(BF)
        sum_push((zz, hf), 4, part.at[hf, for_right], rl.at[u, pl.ds(0, HALF)], right)
        sums[(zz, hf), 1].wait_recv()
        part[hf, for_left] = (part[hf, for_left].astype(F32) + rb[u].astype(F32)).astype(BF)
        sum_push((zz, hf), 5, part.at[hf, for_left], rr.at[u, pl.ds(HALF, HALF)], left)

    crossing = {}

    def cross(hf):
        for i in (2, 3, 4, 5):
            sums[(1, hf), i].wait_recv()
        mine = part[hf, pl.ds(256, BLOCK)].astype(F32)
        zs[hf] = (mine + rl[PARTS + hf].astype(F32) + rr[PARTS + hf].astype(F32)).astype(BF)
        crossing[hf] = push(zs.at[hf], rz.at[hf], zs_sem.at[hf], zr_sem.at[hf], across)

    join(0)
    for hf in range(PARTS):
        partials(0, hf)
        opposite(1, hf)
    join(1)
    for hf in range(PARTS):
        partials(1, hf)
        singles(1, hf)
        doubles(1, hf)
    cross(0)
    join(2)
    for hf in range(PARTS):
        partials(2, hf)
        opposite(0, hf)
        singles(0, hf)
        if hf + 1 < PARTS:
            cross(hf + 1)
    for hf in range(PARTS):
        doubles(0, hf)
    own_rows = pl.ds(0, BLOCK)
    scale = inv[:, pl.ds(0, 1)]
    inner = jnp.zeros((BLOCK, 1), F32)
    for hf in range(PARTS):
        cols = pl.ds(hf * COLS, COLS)
        for i in (2, 3, 4, 5):
            sums[(0, hf), i].wait_recv()
        crossing[hf].wait_recv()
        total = part[hf, own_rows].astype(F32) + rl[hf].astype(F32) + rr[hf].astype(F32) + rz[hf].astype(F32)
        total = total * gain[:, cols]
        inner += jnp.sum(total * (lat[:, cols].astype(F32) * scale), axis=-1, keepdims=True)
        grad[:, cols] = total
    inner = inner * (1.0 / D)
    for hf in range(PARTS):
        cols = pl.ds(hf * COLS, COLS)
        normed = lat[:, cols].astype(F32) * scale
        out_ref[:, cols] = (cot[own_rows, cols].astype(F32) + scale * (grad[:, cols] - normed * inner)).astype(BF)

    for copy in sent:
        copy.wait_send()


def shards(latents, cotangent, norm_gain, w_qkv, w_out):
    hbm = pl.BlockSpec(memory_space=pl.ANY)
    dma = pltpu.SemaphoreType.DMA
    return pl.pallas_call(
        kernel,
        out_shape=jax.ShapeDtypeStruct((BLOCK, D), BF),
        in_specs=[hbm] * 5,
        out_specs=pl.BlockSpec(memory_space=pltpu.VMEM),
        scratch_shapes=[
            pltpu.VMEM((BLOCK, D), BF),
            pltpu.VMEM((1, D), F32),
            pltpu.VMEM((3, D, WIDTH), BF),
            pltpu.VMEM((WIDTH, D), BF),
            pltpu.VMEM((FRAME, D), BF),
            pltpu.VMEM((FRAME, D), BF),
            pltpu.VMEM((BLOCK, 128), F32),
            pltpu.VMEM((FRAME, WIDTH), BF),
            pltpu.VMEM((2 * FRAME, 2 * WIDTH), BF),
            pltpu.VMEM((HEADS_HERE, HEAD_DIM, 2 * FRAME), BF),
            pltpu.VMEM((4 * HEADS_HERE, 2 * FRAME, PAIR), F32),
            pltpu.VMEM((2 * FRAME, WIDTH), F32),
            pltpu.VMEM((2 * FRAME, WIDTH), F32),
            pltpu.VMEM((FRAME, 2 * WIDTH), BF),
            pltpu.VMEM((FRAME, 2 * WIDTH), BF),
            pltpu.VMEM((FRAME, 3 * WIDTH), BF),
            pltpu.VMEM((PARTS, FRAME, COLS), BF),
            pltpu.VMEM((2 * PARTS, HALF, COLS), BF),
            pltpu.VMEM((2 * PARTS, HALF, COLS), BF),
            pltpu.VMEM((2 * PARTS, BLOCK, COLS), BF),
            pltpu.VMEM((2 * PARTS, BLOCK, COLS), BF),
            pltpu.VMEM((PARTS, BLOCK, COLS), BF),
            pltpu.VMEM((PARTS, BLOCK, COLS), BF),
            pltpu.VMEM((PAIR, WIDTH), BF),
            pltpu.VMEM((HEADS_HERE, 2 * FRAME, PAIR), BF),
            pltpu.VMEM((2 * PAIR, WIDTH), BF),
            pltpu.VMEM((2 * FRAME, 2 * PAIR), BF),
            pltpu.VMEM((2 * FRAME, 2 * PAIR), BF),
            pltpu.VMEM((BLOCK, D), F32),
            dma((5,)),
            dma((2, 32)),
            dma((2, 32)),
            dma((4,)),
            dma((4,)),
            dma((3,)),
            dma((3,)),
            dma((12 * PARTS,)),
            dma((12 * PARTS,)),
            dma((PARTS,)),
            dma((PARTS,)),
            pltpu.SemaphoreType.REGULAR,
            pltpu.SemaphoreType.REGULAR,
        ],
        compiler_params=pltpu.CompilerParams(
            collective_id=0, has_side_effects=True, vmem_limit_bytes=56 * 1024 * 1024
        ),
        name="frame_attention_grad",
    )(latents, cotangent, norm_gain.reshape(1, D), jnp.transpose(w_qkv, (1, 0, 2)), w_out)


def solution(mesh):
    return jax.shard_map(
        shards,
        mesh=mesh,
        in_specs=(
            P(("tm", "head"), None),
            P(("tm", "head"), None),
            P(),
            P(None, None, "head"),
            P("head", None),
        ),
        out_specs=P(("tm", "head"), None),
        check_vma=False,
    )
```

```python
import functools

import jax
import jax.numpy as jnp
from jax import lax
from jax.experimental import pallas as pl
from jax.experimental.pallas import tpu as pltpu
from jax.sharding import PartitionSpec as P

EPSILON = 1e-06
MESH = pl.DeviceIdType.MESH
D = 3072
HEAD_DIM = 128
HEADS_HERE = 3
WIDTH = HEADS_HERE * HEAD_DIM
BLOCK = 64
HALF = BLOCK // 2
STEP = BLOCK // 4
FRAME = 512
PAIR = 2 * BLOCK
PARTS = 4
COLS = D // PARTS
N_TM = 32
X = 4
SCALE = HEAD_DIM ** (-0.5)
BF = jnp.bfloat16
F32 = jnp.float32


def nt(a, b):
    return lax.dot_general(a, b, (((1,), (1,)), ((), ())), preferred_element_type=F32)


def nn(a, b):
    return jnp.dot(a, b, preferred_element_type=F32)


def kernel(
    lat_h, cot_h, gain_h, wqkv_h, wout_h, out_h,
    lat, gain, wq, wo, hid, cot, inv, q, kv, kt, probs, acc_k, acc_v, back_s, back_r, g,
    part, ra, rb, rl, rr, zs, rz, ga_s, ds_s, ga_f, ds_f, pb_f, grad,
    ld_sem, gs_sem, gr_sem, kvs_sem, kvr_sem, bs_sem, br_sem, rs_sem, rr_sem, zs_sem, zr_sem, z_ready, tm_ready, out_v, out_sem,
):
    tm = lax.axis_index("tm")
    head = lax.axis_index("head")
    x = lax.rem(head, X)
    base = head - x
    right = (tm, base + lax.rem(x + 1, X))
    left = (tm, base + lax.rem(x + X - 1, X))
    across = (tm, lax.rem(head + X, 2 * X))
    after = (lax.rem(tm + 1, N_TM), head)
    before = (lax.rem(tm + N_TM - 1, N_TM), head)

    barrier = pltpu.get_barrier_semaphore()
    for peer in (right, left, before):
        pl.semaphore_signal(barrier, inc=1, device_id=peer, device_id_type=MESH)

    @pl.when(head < X)
    def _():
        pl.semaphore_signal(barrier, inc=1, device_id=across, device_id_type=MESH)

    loads = [
        pltpu.make_async_copy(lat_h, lat, ld_sem.at[0]),
        pltpu.make_async_copy(gain_h, gain, ld_sem.at[1]),
        pltpu.make_async_copy(cot_h, cot.at[pl.ds(0, BLOCK)], ld_sem.at[2]),
        pltpu.make_async_copy(wqkv_h, wq, ld_sem.at[3]),
        pltpu.make_async_copy(wout_h, wo, ld_sem.at[4]),
    ]
    for load in loads:
        load.start()
    loads[0].wait()
    loads[1].wait()
    for r in range(4):
        rows = pl.ds(r * 16, 16)
        lf = lat[rows].astype(F32)
        scale = lax.rsqrt(jnp.mean(lf * lf, axis=-1, keepdims=True) + EPSILON)
        inv[rows] = jnp.broadcast_to(scale, (16, 128))
        hid[rows] = (lf * scale * gain[...]).astype(BF)
    @pl.when(head < X)
    def _():
        pl.semaphore_wait(barrier, 3)

    @pl.when(head >= X)
    def _():
        pl.semaphore_wait(barrier, 4)
        pl.semaphore_signal(z_ready, inc=1, device_id=across, device_id_type=MESH)

    pl.semaphore_signal(tm_ready, inc=1, device_id=after, device_id_type=MESH)

    sent = []

    def push(src, dst, s_sem, r_sem, peer):
        copy = pltpu.make_async_remote_copy(
            src_ref=src, dst_ref=dst, send_sem=s_sem, recv_sem=r_sem, device_id=peer, device_id_type=MESH
        )
        copy.start()
        sent.append(copy)
        return copy

    def settle(n):
        for copy in sent[:n]:
            copy.wait_send()
        del sent[:n]

    def chunk(slot, c):
        return pl.ds(slot * BLOCK + c * HALF, HALF)

    bufs = (hid, cot)
    moves = {}

    def gather_push(a, src_slot, dst_slot, c, peer):
        i = dst_slot * 4 + c
        moves[a, dst_slot, c] = push(
            bufs[a].at[pl.ds(src_slot * BLOCK + c * STEP, STEP)], bufs[a].at[pl.ds(dst_slot * BLOCK + c * STEP, STEP)],
            gs_sem.at[a, i], gr_sem.at[a, i], peer,
        )

    def got(a, slot, cs=(0, 1, 2, 3)):
        for c in cs:
            moves[a, slot, c].wait_recv()

    def to_right(a, zz, c):
        gather_push(a, 4 * zz, 4 * zz + 1, c, right)

    def to_left(a, zz, c):
        gather_push(a, 4 * zz, 4 * zz + 2, c, left)

    def spread(a, c):
        got(a, 4, (c,))
        to_right(a, 1, c)
        to_left(a, 1, c)

    def forward(a, zz, c):
        near = 4 * zz + 1 + c % 2
        got(a, near, (c,))
        gather_push(a, near, 4 * zz + 3, c, left if c % 2 else right)

    kv_copies = []

    def project(p):
        rows = pl.ds(p * PAIR, PAIR)
        h = hid[rows]
        q[rows] = nn(h, wq[0]).astype(BF)
        kv[rows, pl.ds(0, WIDTH)] = nn(h, wq[1]).astype(BF)
        kv[rows, pl.ds(WIDTH, WIDTH)] = nn(h, wq[2]).astype(BF)
        kv_copies.append(
            push(kv.at[rows], kv.at[pl.ds(FRAME + p * PAIR, PAIR)], kvs_sem.at[p], kvr_sem.at[p], after)
        )

    for c in range(4):
        to_right(0, 0, (0, 2, 1, 3)[c])
        to_left(0, 0, (1, 3, 0, 2)[c])

    @pl.when(head < X)
    def _():
        pl.semaphore_wait(z_ready, 1)

    for c in range(4):
        gather_push(0, 0, 4, c, across)
    loads[2].wait()
    for c in range(4):
        forward(0, 0, c)
        (to_left if c % 2 else to_right)(1, 0, c)
    loads[3].wait()
    got(0, 1, (1, 3))
    project(0)
    spread(0, 0)
    spread(0, 1)
    for c in range(4):
        (to_right if c % 2 else to_left)(1, 0, c)
    got(0, 2, (0, 2))
    got(0, 3)
    project(1)
    spread(0, 2)
    for c in range(4):
        gather_push(1, 0, 4, c, across)
    spread(0, 3)
    for c in range(4):
        forward(0, 1, c)
    for c in range(4):
        forward(1, 0, c)
    got(0, 5, (1, 3))
    project(2)
    spread(1, 0)
    got(0, 6, (0, 2))
    got(0, 7)
    project(3)
    spread(1, 1)
    loads[4].wait()

    def lanes(h):
        if isinstance(h, int):
            return pl.ds(h * HEAD_DIM, HEAD_DIM)
        return pl.ds(pl.multiple_of(h * HEAD_DIM, HEAD_DIM), HEAD_DIM)

    def v_lanes(h):
        if isinstance(h, int):
            return pl.ds(WIDTH + h * HEAD_DIM, HEAD_DIM)
        return pl.ds(pl.multiple_of(WIDTH + h * HEAD_DIM, HEAD_DIM), HEAD_DIM)

    def turn(rows):
        def one(h, carry):
            kt[h, :, rows] = kv[rows, lanes(h)].astype(F32).T.astype(BF)
            return carry

        lax.fori_loop(0, HEADS_HERE, one, 0)

    own = pl.ds(0, FRAME)
    prev = pl.ds(FRAME, FRAME)

    def queries_of(i):
        p = i // HEADS_HERE
        h = i - p * HEADS_HERE
        return h, q[pl.ds(pl.multiple_of(p * PAIR, PAIR), PAIR), lanes(h)]

    def score_own(i, carry):
        h, qh = queries_of(i)
        probs[i, own] = nt(kv[own, lanes(h)], qh) * SCALE
        return carry

    def score(i, carry):
        h, qh = queries_of(i)
        own_s = probs[i, own]
        prev_s = jnp.where(tm > 0, nt(kv[prev, lanes(h)], qh) * SCALE, -1e30)
        top = jnp.maximum(jnp.max(own_s, axis=0, keepdims=True), jnp.max(prev_s, axis=0, keepdims=True))
        own_e = jnp.exp(own_s - top)
        prev_e = jnp.exp(prev_s - top)
        part_of = 1.0 / (jnp.sum(own_e, axis=0, keepdims=True) + jnp.sum(prev_e, axis=0, keepdims=True))
        probs[i, own] = own_e * part_of
        probs[i, prev] = prev_e * part_of
        return carry

    lax.fori_loop(0, 4 * HEADS_HERE, score_own, 0)
    turn(own)
    got(1, 1, (1, 3))
    got(1, 2, (0, 2))
    got(1, 3)
    for p in (0, 1):
        ga_f[pl.ds(p * PAIR, PAIR)] = nt(cot[pl.ds(p * PAIR, PAIR)], wo[...]).astype(BF)
    for copy in kv_copies:
        copy.wait_recv()
    turn(prev)

    lax.fori_loop(0, 2 * HEADS_HERE, score, 0)
    spread(1, 2)
    lax.fori_loop(2 * HEADS_HERE, 4 * HEADS_HERE, score, 0)

    def score_grads(p, h):
        pt = probs[p * HEADS_HERE + h]
        dp = nt(kv[:, v_lanes(h)], ga_s[:, lanes(h)])
        delta = jnp.sum(pt * dp, axis=0, keepdims=True)
        return pt, (pt * (dp - delta) * SCALE).astype(BF)

    def backward(p):
        rows = pl.ds(p * PAIR, PAIR)
        ga_s[...] = nt(cot[rows], wo[...]).astype(BF)

        def one(h, carry):
            pt, ds = score_grads(p, h)
            acc_k[:, lanes(h)] += nn(ds, q[rows, lanes(h)])
            acc_v[:, lanes(h)] += nn(pt.astype(BF), ga_s[:, lanes(h)])
            g[rows, lanes(h)] = nn(kt[h], ds).T.astype(BF)
            return carry

        lax.fori_loop(0, HEADS_HERE, one, 0)


    def backward_first(h):
        rows = pl.ds(0, 2 * PAIR)
        dp = nt(kv[:, v_lanes(h)], ga_f[:, lanes(h)])
        for p in (0, 1):
            pt = probs[p * HEADS_HERE + h]
            dpp = dp[:, p * PAIR : (p + 1) * PAIR]
            delta = jnp.sum(pt * dpp, axis=0, keepdims=True)
            ds_f[:, pl.ds(p * PAIR, PAIR)] = (pt * (dpp - delta) * SCALE).astype(BF)
            pb_f[:, pl.ds(p * PAIR, PAIR)] = pt.astype(BF)
        acc_k[:, lanes(h)] = nn(ds_f[...], q[rows, lanes(h)])
        acc_v[:, lanes(h)] = nn(pb_f[...], ga_f[:, lanes(h)])
        g[rows, lanes(h)] = nn(kt[h], ds_f[...]).T.astype(BF)

    forward(1, 1, 0)
    forward(1, 1, 1)
    backward_first(0)
    spread(1, 3)
    backward_first(1)
    forward(1, 1, 2)
    backward_first(2)
    forward(1, 1, 3)
    got(1, 5, (1, 3))
    backward(2)
    got(1, 6, (0, 2))
    got(1, 7)

    last = pl.ds(3 * PAIR, PAIR)
    ga_s[...] = nt(cot[last], wo[...]).astype(BF)

    def last_prev(h, carry):
        pt, ds = score_grads(3, h)
        ds_s[h] = ds
        back_piece(h, *pieces[0])
        return carry

    def back_piece(h, start, size):
        theirs = pl.ds(FRAME + start, size)
        ours = pl.ds(start, size)
        weights = probs[3 * HEADS_HERE + h, theirs].astype(BF)
        back_s[ours, lanes(h)] = (acc_k[theirs, lanes(h)] + nn(ds_s[h, theirs], q[last, lanes(h)])).astype(BF)
        back_s[ours, v_lanes(h)] = (acc_v[theirs, lanes(h)] + nn(weights, ga_s[:, lanes(h)])).astype(BF)

    pieces = ((448, 64), (256, 192), (0, 256))
    n_gather = len(sent)
    backs = []

    def send_back(i):
        rows = pl.ds(*pieces[i])
        backs.append(push(back_s.at[rows], back_r.at[rows], bs_sem.at[i], br_sem.at[i], before))

    lax.fori_loop(0, HEADS_HERE, last_prev, 0)
    pl.semaphore_wait(tm_ready, 1)
    send_back(0)
    for i in (1, 2):

        def rest(h, carry):
            back_piece(h, *pieces[i])
            return carry

        lax.fori_loop(0, HEADS_HERE, rest, 0)
        send_back(i)

    def last_own(h, carry):
        g[last, lanes(h)] = nn(kt[h], ds_s[h]).T.astype(BF)
        acc_k[own, lanes(h)] += nn(ds_s[h, own], q[last, lanes(h)])
        acc_v[own, lanes(h)] += nn(probs[3 * HEADS_HERE + h, own].astype(BF), ga_s[:, lanes(h)])
        return carry

    lax.fori_loop(0, HEADS_HERE, last_own, 0)

    def join(i):
        rows = pl.ds(*pieces[i])
        backs[i].wait_recv()
        g[rows, pl.ds(WIDTH, WIDTH)] = (acc_k[rows] + back_r[rows, pl.ds(0, WIDTH)].astype(F32)).astype(BF)
        g[rows, pl.ds(2 * WIDTH, WIDTH)] = (acc_v[rows] + back_r[rows, pl.ds(WIDTH, WIDTH)].astype(F32)).astype(BF)

    def partials(i, hf):
        rows = pl.ds(*pieces[i])

        def tile(n, carry):
            w_rows = pl.ds(pl.multiple_of(hf * COLS + n * 384, 128), 384)
            total = nt(g[rows, pl.ds(0, WIDTH)], wq[0, w_rows])
            total += nt(g[rows, pl.ds(WIDTH, WIDTH)], wq[1, w_rows])
            total += nt(g[rows, pl.ds(2 * WIDTH, WIDTH)], wq[2, w_rows])
            part[hf, rows, pl.ds(pl.multiple_of(n * 384, 128), 384)] = total.astype(BF)
            return carry

        lax.fori_loop(0, COLS // 384, tile, 0)

    sums = {}

    def sum_push(key, i, src, dst, peer):
        zz, hf = key
        k = (zz * PARTS + hf) * 6 + i
        sums[key, i] = push(src, dst, rs_sem.at[k], rr_sem.at[k], peer)

    def opposite(zz, hf):
        u = zz * PARTS + hf
        sum_push((zz, hf), 0, part.at[hf, chunk(4 * zz + 3, 0)], ra.at[u], right)
        sum_push((zz, hf), 1, part.at[hf, chunk(4 * zz + 3, 1)], rb.at[u], left)

    def singles(zz, hf):
        u = zz * PARTS + hf
        sum_push((zz, hf), 2, part.at[hf, chunk(4 * zz + 2, 1)], rl.at[u, pl.ds(HALF, HALF)], right)
        sum_push((zz, hf), 3, part.at[hf, chunk(4 * zz + 1, 0)], rr.at[u, pl.ds(0, HALF)], left)

    def doubles(zz, hf):
        u = zz * PARTS + hf
        for_right = chunk(4 * zz + 2, 0)
        for_left = chunk(4 * zz + 1, 1)
        sums[(zz, hf), 0].wait_recv()
        part[hf, for_right] = (part[hf, for_right].astype(F32) + ra[u].astype(F32)).astype(BF)
        sum_push((zz, hf), 4, part.at[hf, for_right], rl.at[u, pl.ds(0, HALF)], right)
        sums[(zz, hf), 1].wait_recv()
        part[hf, for_left] = (part[hf, for_left].astype(F32) + rb[u].astype(F32)).astype(BF)
        sum_push((zz, hf), 5, part.at[hf, for_left], rr.at[u, pl.ds(HALF, HALF)], left)

    crossing = {}

    def cross(hf):
        for i in (2, 3, 4, 5):
            sums[(1, hf), i].wait_recv()
        mine = part[hf, pl.ds(256, BLOCK)].astype(F32)
        zs[hf] = (mine + rl[PARTS + hf].astype(F32) + rr[PARTS + hf].astype(F32)).astype(BF)
        crossing[hf] = push(zs.at[hf], rz.at[hf], zs_sem.at[hf], zr_sem.at[hf], across)

    settle(n_gather)
    join(0)
    for hf in range(PARTS):
        partials(0, hf)
        opposite(1, hf)
    join(1)
    for hf in range(PARTS):
        partials(1, hf)
        singles(1, hf)
        doubles(1, hf)
    n_first = len(sent)
    cross(0)
    join(2)
    for hf in range(PARTS):
        partials(2, hf)
        opposite(0, hf)
        singles(0, hf)
        if hf + 1 < PARTS:
            cross(hf + 1)
    for hf in range(PARTS):
        doubles(0, hf)
    settle(n_first)
    own_rows = pl.ds(0, BLOCK)
    scale = inv[:, pl.ds(0, 1)]
    inner = jnp.zeros((BLOCK, 1), F32)
    for hf in range(PARTS):
        cols = pl.ds(hf * COLS, COLS)
        for i in (2, 3, 4, 5):
            sums[(0, hf), i].wait_recv()
        crossing[hf].wait_recv()
        total = part[hf, own_rows].astype(F32) + rl[hf].astype(F32) + rr[hf].astype(F32) + rz[hf].astype(F32)
        total = total * gain[:, cols]
        inner += jnp.sum(total * (lat[:, cols].astype(F32) * scale), axis=-1, keepdims=True)
        grad[:, cols] = total
    inner = inner * (1.0 / D)
    outs = []
    for hf in range(PARTS):
        cols = pl.ds(hf * COLS, COLS)
        normed = lat[:, cols].astype(F32) * scale
        out_v[hf] = (cot[own_rows, cols].astype(F32) + scale * (grad[:, cols] - normed * inner)).astype(BF)
        outs.append(pltpu.make_async_copy(out_v.at[hf], out_h.at[:, cols], out_sem.at[hf]))
        outs[-1].start()

    settle(len(sent))
    for copy in outs:
        copy.wait()


def shards(latents, cotangent, norm_gain, w_qkv, w_out):
    hbm = pl.BlockSpec(memory_space=pl.ANY)
    dma = pltpu.SemaphoreType.DMA
    return pl.pallas_call(
        kernel,
        out_shape=jax.ShapeDtypeStruct((BLOCK, D), BF),
        in_specs=[hbm] * 5,
        out_specs=hbm,
        scratch_shapes=[
            pltpu.VMEM((BLOCK, D), BF),
            pltpu.VMEM((1, D), F32),
            pltpu.VMEM((3, D, WIDTH), BF),
            pltpu.VMEM((WIDTH, D), BF),
            pltpu.VMEM((FRAME, D), BF),
            pltpu.VMEM((FRAME, D), BF),
            pltpu.VMEM((BLOCK, 128), F32),
            pltpu.VMEM((FRAME, WIDTH), BF),
            pltpu.VMEM((2 * FRAME, 2 * WIDTH), BF),
            pltpu.VMEM((HEADS_HERE, HEAD_DIM, 2 * FRAME), BF),
            pltpu.VMEM((4 * HEADS_HERE, 2 * FRAME, PAIR), F32),
            pltpu.VMEM((2 * FRAME, WIDTH), F32),
            pltpu.VMEM((2 * FRAME, WIDTH), F32),
            pltpu.VMEM((FRAME, 2 * WIDTH), BF),
            pltpu.VMEM((FRAME, 2 * WIDTH), BF),
            pltpu.VMEM((FRAME, 3 * WIDTH), BF),
            pltpu.VMEM((PARTS, FRAME, COLS), BF),
            pltpu.VMEM((2 * PARTS, HALF, COLS), BF),
            pltpu.VMEM((2 * PARTS, HALF, COLS), BF),
            pltpu.VMEM((2 * PARTS, BLOCK, COLS), BF),
            pltpu.VMEM((2 * PARTS, BLOCK, COLS), BF),
            pltpu.VMEM((PARTS, BLOCK, COLS), BF),
            pltpu.VMEM((PARTS, BLOCK, COLS), BF),
            pltpu.VMEM((PAIR, WIDTH), BF),
            pltpu.VMEM((HEADS_HERE, 2 * FRAME, PAIR), BF),
            pltpu.VMEM((2 * PAIR, WIDTH), BF),
            pltpu.VMEM((2 * FRAME, 2 * PAIR), BF),
            pltpu.VMEM((2 * FRAME, 2 * PAIR), BF),
            pltpu.VMEM((BLOCK, D), F32),
            dma((5,)),
            dma((2, 32)),
            dma((2, 32)),
            dma((4,)),
            dma((4,)),
            dma((3,)),
            dma((3,)),
            dma((12 * PARTS,)),
            dma((12 * PARTS,)),
            dma((PARTS,)),
            dma((PARTS,)),
            pltpu.SemaphoreType.REGULAR,
            pltpu.SemaphoreType.REGULAR,
            pltpu.VMEM((PARTS, BLOCK, COLS), BF),
            dma((PARTS,)),
        ],
        compiler_params=pltpu.CompilerParams(
            collective_id=0, has_side_effects=True, vmem_limit_bytes=56 * 1024 * 1024
        ),
        name="frame_attention_grad",
    )(latents, cotangent, norm_gain.reshape(1, D), jnp.transpose(w_qkv, (1, 0, 2)), w_out)


def solution(mesh):
    return jax.shard_map(
        shards,
        mesh=mesh,
        in_specs=(
            P(("tm", "head"), None),
            P(("tm", "head"), None),
            P(),
            P(None, None, "head"),
            P("head", None),
        ),
        out_specs=P(("tm", "head"), None),
        check_vma=False,
    )
```

```python
import functools

import jax
import jax.numpy as jnp
from jax import lax
from jax.experimental import pallas as pl
from jax.experimental.pallas import tpu as pltpu
from jax.sharding import PartitionSpec as P

EPSILON = 1e-06
MESH = pl.DeviceIdType.MESH
D = 3072
HEAD_DIM = 128
HEADS_HERE = 3
WIDTH = HEADS_HERE * HEAD_DIM
BLOCK = 64
HALF = BLOCK // 2
STEP = BLOCK // 4
FRAME = 512
PAIR = 2 * BLOCK
PARTS = 4
COLS = D // PARTS
N_TM = 32
X = 4
SCALE = HEAD_DIM ** (-0.5)
BF = jnp.bfloat16
F32 = jnp.float32


def nt(a, b):
    return lax.dot_general(a, b, (((1,), (1,)), ((), ())), preferred_element_type=F32)


def nn(a, b):
    return jnp.dot(a, b, preferred_element_type=F32)


def kernel(
    lat_h, cot_h, gain_h, wqkv_h, wout_h, out_h,
    lat, gain, wq, wo, hid, cot, inv, q, kv, kt, probs, acc_k, acc_v, back_s, back_r, g,
    part, ra, rb, rl, rr, zs, rz, ga_s, ds_s, ga_f, ds_f, pb_f, grad,
    ld_sem, gs_sem, gr_sem, kvs_sem, kvr_sem, bs_sem, br_sem, rs_sem, rr_sem, zs_sem, zr_sem, z_ready, tm_ready, out_v, out_sem,
):
    tm = lax.axis_index("tm")
    head = lax.axis_index("head")
    x = lax.rem(head, X)
    base = head - x
    right = (tm, base + lax.rem(x + 1, X))
    left = (tm, base + lax.rem(x + X - 1, X))
    across = (tm, lax.rem(head + X, 2 * X))
    after = (lax.rem(tm + 1, N_TM), head)
    before = (lax.rem(tm + N_TM - 1, N_TM), head)

    barrier = pltpu.get_barrier_semaphore()
    for peer in (right, left, before):
        pl.semaphore_signal(barrier, inc=1, device_id=peer, device_id_type=MESH)

    @pl.when(head < X)
    def _():
        pl.semaphore_signal(barrier, inc=1, device_id=across, device_id_type=MESH)

    loads = [
        pltpu.make_async_copy(lat_h, lat, ld_sem.at[0]),
        pltpu.make_async_copy(gain_h, gain, ld_sem.at[1]),
        pltpu.make_async_copy(cot_h, cot.at[pl.ds(0, BLOCK)], ld_sem.at[2]),
        pltpu.make_async_copy(wqkv_h, wq, ld_sem.at[3]),
        pltpu.make_async_copy(wout_h, wo, ld_sem.at[4]),
    ]
    for load in loads:
        load.start()
    loads[0].wait()
    loads[1].wait()
    for r in range(4):
        rows = pl.ds(r * 16, 16)
        lf = lat[rows].astype(F32)
        scale = lax.rsqrt(jnp.mean(lf * lf, axis=-1, keepdims=True) + EPSILON)
        inv[rows] = jnp.broadcast_to(scale, (16, 128))
        hid[rows] = (lf * scale * gain[...]).astype(BF)
    @pl.when(head < X)
    def _():
        pl.semaphore_wait(barrier, 3)

    @pl.when(head >= X)
    def _():
        pl.semaphore_wait(barrier, 4)
        pl.semaphore_signal(z_ready, inc=1, device_id=across, device_id_type=MESH)

    pl.semaphore_signal(tm_ready, inc=1, device_id=after, device_id_type=MESH)

    sent = []

    def push(src, dst, s_sem, r_sem, peer):
        copy = pltpu.make_async_remote_copy(
            src_ref=src, dst_ref=dst, send_sem=s_sem, recv_sem=r_sem, device_id=peer, device_id_type=MESH
        )
        copy.start()
        sent.append(copy)
        return copy

    def settle(n):
        for copy in sent[:n]:
            copy.wait_send()
        del sent[:n]

    def chunk(slot, c):
        return pl.ds(slot * BLOCK + c * HALF, HALF)

    bufs = (hid, cot)
    moves = {}

    def gather_push(a, src_slot, dst_slot, c, peer):
        i = dst_slot * 4 + c
        moves[a, dst_slot, c] = push(
            bufs[a].at[pl.ds(src_slot * BLOCK + c * STEP, STEP)], bufs[a].at[pl.ds(dst_slot * BLOCK + c * STEP, STEP)],
            gs_sem.at[a, i], gr_sem.at[a, i], peer,
        )

    def got(a, slot, cs=(0, 1, 2, 3)):
        for c in cs:
            moves[a, slot, c].wait_recv()

    def to_right(a, zz, c):
        gather_push(a, 4 * zz, 4 * zz + 1, c, right)

    def to_left(a, zz, c):
        gather_push(a, 4 * zz, 4 * zz + 2, c, left)

    def spread(a, c):
        got(a, 4, (c,))
        to_right(a, 1, c)
        to_left(a, 1, c)

    def forward(a, zz, c):
        near = 4 * zz + 1 + c % 2
        got(a, near, (c,))
        gather_push(a, near, 4 * zz + 3, c, left if c % 2 else right)

    kv_copies = []

    def project(p):
        rows = pl.ds(p * PAIR, PAIR)
        h = hid[rows]
        q[rows] = nn(h, wq[0]).astype(BF)
        kv[rows, pl.ds(0, WIDTH)] = nn(h, wq[1]).astype(BF)
        kv[rows, pl.ds(WIDTH, WIDTH)] = nn(h, wq[2]).astype(BF)
        kv_copies.append(
            push(kv.at[rows], kv.at[pl.ds(FRAME + p * PAIR, PAIR)], kvs_sem.at[p], kvr_sem.at[p], after)
        )

    for c in range(4):
        to_right(0, 0, (0, 2, 1, 3)[c])
        to_left(0, 0, (1, 3, 0, 2)[c])

    @pl.when(head < X)
    def _():
        pl.semaphore_wait(z_ready, 1)

    for c in range(4):
        gather_push(0, 0, 4, c, across)
    loads[2].wait()
    for c in range(4):
        forward(0, 0, c)
        (to_left if c % 2 else to_right)(1, 0, c)
    loads[3].wait()
    got(0, 1, (1, 3))
    project(0)
    spread(0, 0)
    spread(0, 1)
    for c in range(4):
        (to_right if c % 2 else to_left)(1, 0, c)
    got(0, 2, (0, 2))
    got(0, 3)
    project(1)
    for c in range(4):
        gather_push(1, 0, 4, c, across)
    spread(0, 2)
    spread(0, 3)
    for c in range(4):
        forward(0, 1, c)
    for c in range(4):
        forward(1, 0, c)
    got(0, 5, (1, 3))
    project(2)
    spread(1, 0)
    got(0, 6, (0, 2))
    got(0, 7)
    project(3)
    spread(1, 1)
    loads[4].wait()

    def lanes(h):
        if isinstance(h, int):
            return pl.ds(h * HEAD_DIM, HEAD_DIM)
        return pl.ds(pl.multiple_of(h * HEAD_DIM, HEAD_DIM), HEAD_DIM)

    def v_lanes(h):
        if isinstance(h, int):
            return pl.ds(WIDTH + h * HEAD_DIM, HEAD_DIM)
        return pl.ds(pl.multiple_of(WIDTH + h * HEAD_DIM, HEAD_DIM), HEAD_DIM)

    def turn(rows):
        def one(h, carry):
            kt[h, :, rows] = kv[rows, lanes(h)].astype(F32).T.astype(BF)
            return carry

        lax.fori_loop(0, HEADS_HERE, one, 0)

    own = pl.ds(0, FRAME)
    prev = pl.ds(FRAME, FRAME)

    def queries_of(i):
        p = i // HEADS_HERE
        h = i - p * HEADS_HERE
        return h, q[pl.ds(pl.multiple_of(p * PAIR, PAIR), PAIR), lanes(h)]

    def score_own(i, carry):
        h, qh = queries_of(i)
        probs[i, own] = nt(kv[own, lanes(h)], qh) * SCALE
        return carry

    def score(i, carry):
        h, qh = queries_of(i)
        own_s = probs[i, own]
        prev_s = jnp.where(tm > 0, nt(kv[prev, lanes(h)], qh) * SCALE, -1e30)
        top = jnp.maximum(jnp.max(own_s, axis=0, keepdims=True), jnp.max(prev_s, axis=0, keepdims=True))
        own_e = jnp.exp(own_s - top)
        prev_e = jnp.exp(prev_s - top)
        part_of = 1.0 / (jnp.sum(own_e, axis=0, keepdims=True) + jnp.sum(prev_e, axis=0, keepdims=True))
        probs[i, own] = own_e * part_of
        probs[i, prev] = prev_e * part_of
        return carry

    lax.fori_loop(0, 4 * HEADS_HERE, score_own, 0)
    turn(own)
    got(1, 1, (1, 3))
    got(1, 2, (0, 2))
    got(1, 3)
    for p in (0, 1):
        ga_f[pl.ds(p * PAIR, PAIR)] = nt(cot[pl.ds(p * PAIR, PAIR)], wo[...]).astype(BF)
    for copy in kv_copies:
        copy.wait_recv()
    turn(prev)

    lax.fori_loop(0, 2 * HEADS_HERE, score, 0)
    spread(1, 2)
    lax.fori_loop(2 * HEADS_HERE, 4 * HEADS_HERE, score, 0)

    def score_grads(p, h):
        pt = probs[p * HEADS_HERE + h]
        dp = nt(kv[:, v_lanes(h)], ga_s[:, lanes(h)])
        delta = jnp.sum(pt * dp, axis=0, keepdims=True)
        return pt, (pt * (dp - delta) * SCALE).astype(BF)

    def backward(p):
        rows = pl.ds(p * PAIR, PAIR)
        ga_s[...] = nt(cot[rows], wo[...]).astype(BF)

        def one(h, carry):
            pt, ds = score_grads(p, h)
            acc_k[:, lanes(h)] += nn(ds, q[rows, lanes(h)])
            acc_v[:, lanes(h)] += nn(pt.astype(BF), ga_s[:, lanes(h)])
            g[rows, lanes(h)] = nn(kt[h], ds).T.astype(BF)
            return carry

        lax.fori_loop(0, HEADS_HERE, one, 0)


    def backward_first(h):
        rows = pl.ds(0, 2 * PAIR)
        dp = nt(kv[:, v_lanes(h)], ga_f[:, lanes(h)])
        for p in (0, 1):
            pt = probs[p * HEADS_HERE + h]
            dpp = dp[:, p * PAIR : (p + 1) * PAIR]
            delta = jnp.sum(pt * dpp, axis=0, keepdims=True)
            ds_f[:, pl.ds(p * PAIR, PAIR)] = (pt * (dpp - delta) * SCALE).astype(BF)
            pb_f[:, pl.ds(p * PAIR, PAIR)] = pt.astype(BF)
        acc_k[:, lanes(h)] = nn(ds_f[...], q[rows, lanes(h)])
        acc_v[:, lanes(h)] = nn(pb_f[...], ga_f[:, lanes(h)])
        g[rows, lanes(h)] = nn(kt[h], ds_f[...]).T.astype(BF)

    forward(1, 1, 0)
    forward(1, 1, 1)
    backward_first(0)
    spread(1, 3)
    backward_first(1)
    forward(1, 1, 2)
    backward_first(2)
    forward(1, 1, 3)
    got(1, 5, (1, 3))
    backward(2)
    got(1, 6, (0, 2))
    got(1, 7)

    last = pl.ds(3 * PAIR, PAIR)
    ga_s[...] = nt(cot[last], wo[...]).astype(BF)

    def last_prev(h, carry):
        pt, ds = score_grads(3, h)
        ds_s[h] = ds
        back_piece(h, *pieces[0])
        return carry

    def back_piece(h, start, size):
        theirs = pl.ds(FRAME + start, size)
        ours = pl.ds(start, size)
        weights = probs[3 * HEADS_HERE + h, theirs].astype(BF)
        back_s[ours, lanes(h)] = (acc_k[theirs, lanes(h)] + nn(ds_s[h, theirs], q[last, lanes(h)])).astype(BF)
        back_s[ours, v_lanes(h)] = (acc_v[theirs, lanes(h)] + nn(weights, ga_s[:, lanes(h)])).astype(BF)

    pieces = ((448, 64), (256, 192), (0, 256))
    n_gather = len(sent)
    backs = []

    def send_back(i):
        rows = pl.ds(*pieces[i])
        backs.append(push(back_s.at[rows], back_r.at[rows], bs_sem.at[i], br_sem.at[i], before))

    lax.fori_loop(0, HEADS_HERE, last_prev, 0)
    pl.semaphore_wait(tm_ready, 1)
    send_back(0)
    for i in (1, 2):

        def rest(h, carry):
            back_piece(h, *pieces[i])
            return carry

        lax.fori_loop(0, HEADS_HERE, rest, 0)
        send_back(i)

    def last_own(h, carry):
        g[last, lanes(h)] = nn(kt[h], ds_s[h]).T.astype(BF)
        acc_k[own, lanes(h)] += nn(ds_s[h, own], q[last, lanes(h)])
        acc_v[own, lanes(h)] += nn(probs[3 * HEADS_HERE + h, own].astype(BF), ga_s[:, lanes(h)])
        return carry

    lax.fori_loop(0, HEADS_HERE, last_own, 0)

    def join(i):
        rows = pl.ds(*pieces[i])
        backs[i].wait_recv()
        g[rows, pl.ds(WIDTH, WIDTH)] = (acc_k[rows] + back_r[rows, pl.ds(0, WIDTH)].astype(F32)).astype(BF)
        g[rows, pl.ds(2 * WIDTH, WIDTH)] = (acc_v[rows] + back_r[rows, pl.ds(WIDTH, WIDTH)].astype(F32)).astype(BF)

    def partials(i, hf):
        rows = pl.ds(*pieces[i])

        def tile(n, carry):
            w_rows = pl.ds(pl.multiple_of(hf * COLS + n * 384, 128), 384)
            total = nt(g[rows, pl.ds(0, WIDTH)], wq[0, w_rows])
            total += nt(g[rows, pl.ds(WIDTH, WIDTH)], wq[1, w_rows])
            total += nt(g[rows, pl.ds(2 * WIDTH, WIDTH)], wq[2, w_rows])
            part[hf, rows, pl.ds(pl.multiple_of(n * 384, 128), 384)] = total.astype(BF)
            return carry

        lax.fori_loop(0, COLS // 384, tile, 0)

    sums = {}

    def sum_push(key, i, src, dst, peer):
        zz, hf = key
        k = (zz * PARTS + hf) * 6 + i
        sums[key, i] = push(src, dst, rs_sem.at[k], rr_sem.at[k], peer)

    def opposite(zz, hf):
        u = zz * PARTS + hf
        sum_push((zz, hf), 0, part.at[hf, chunk(4 * zz + 3, 0)], ra.at[u], right)
        sum_push((zz, hf), 1, part.at[hf, chunk(4 * zz + 3, 1)], rb.at[u], left)

    def singles(zz, hf):
        u = zz * PARTS + hf
        sum_push((zz, hf), 2, part.at[hf, chunk(4 * zz + 2, 1)], rl.at[u, pl.ds(HALF, HALF)], right)
        sum_push((zz, hf), 3, part.at[hf, chunk(4 * zz + 1, 0)], rr.at[u, pl.ds(0, HALF)], left)

    def doubles(zz, hf):
        u = zz * PARTS + hf
        for_right = chunk(4 * zz + 2, 0)
        for_left = chunk(4 * zz + 1, 1)
        sums[(zz, hf), 0].wait_recv()
        part[hf, for_right] = (part[hf, for_right].astype(F32) + ra[u].astype(F32)).astype(BF)
        sum_push((zz, hf), 4, part.at[hf, for_right], rl.at[u, pl.ds(0, HALF)], right)
        sums[(zz, hf), 1].wait_recv()
        part[hf, for_left] = (part[hf, for_left].astype(F32) + rb[u].astype(F32)).astype(BF)
        sum_push((zz, hf), 5, part.at[hf, for_left], rr.at[u, pl.ds(HALF, HALF)], left)

    crossing = {}

    def cross(hf):
        for i in (2, 3, 4, 5):
            sums[(1, hf), i].wait_recv()
        mine = part[hf, pl.ds(256, BLOCK)].astype(F32)
        zs[hf] = (mine + rl[PARTS + hf].astype(F32) + rr[PARTS + hf].astype(F32)).astype(BF)
        crossing[hf] = push(zs.at[hf], rz.at[hf], zs_sem.at[hf], zr_sem.at[hf], across)

    settle(n_gather)
    join(0)
    for hf in range(PARTS):
        partials(0, hf)
        opposite(1, hf)
    join(1)
    for hf in range(PARTS):
        partials(1, hf)
        singles(1, hf)
        doubles(1, hf)
    n_first = len(sent)
    cross(0)
    join(2)
    for hf in range(PARTS):
        partials(2, hf)
        opposite(0, hf)
        singles(0, hf)
        if hf + 1 < PARTS:
            cross(hf + 1)
    for hf in range(PARTS):
        doubles(0, hf)
    settle(n_first)
    own_rows = pl.ds(0, BLOCK)
    scale = inv[:, pl.ds(0, 1)]
    inner = jnp.zeros((BLOCK, 1), F32)
    for hf in range(PARTS):
        cols = pl.ds(hf * COLS, COLS)
        for i in (2, 3, 4, 5):
            sums[(0, hf), i].wait_recv()
        crossing[hf].wait_recv()
        total = part[hf, own_rows].astype(F32) + rl[hf].astype(F32) + rr[hf].astype(F32) + rz[hf].astype(F32)
        total = total * gain[:, cols]
        inner += jnp.sum(total * (lat[:, cols].astype(F32) * scale), axis=-1, keepdims=True)
        grad[:, cols] = total
    inner = inner * (1.0 / D)
    outs = []
    for hf in range(PARTS):
        cols = pl.ds(hf * COLS, COLS)
        normed = lat[:, cols].astype(F32) * scale
        out_v[hf] = (cot[own_rows, cols].astype(F32) + scale * (grad[:, cols] - normed * inner)).astype(BF)
        outs.append(pltpu.make_async_copy(out_v.at[hf], out_h.at[:, cols], out_sem.at[hf]))
        outs[-1].start()

    settle(len(sent))
    for copy in outs:
        copy.wait()


def shards(latents, cotangent, norm_gain, w_qkv, w_out):
    hbm = pl.BlockSpec(memory_space=pl.ANY)
    dma = pltpu.SemaphoreType.DMA
    return pl.pallas_call(
        kernel,
        out_shape=jax.ShapeDtypeStruct((BLOCK, D), BF),
        in_specs=[hbm] * 5,
        out_specs=hbm,
        scratch_shapes=[
            pltpu.VMEM((BLOCK, D), BF),
            pltpu.VMEM((1, D), F32),
            pltpu.VMEM((3, D, WIDTH), BF),
            pltpu.VMEM((WIDTH, D), BF),
            pltpu.VMEM((FRAME, D), BF),
            pltpu.VMEM((FRAME, D), BF),
            pltpu.VMEM((BLOCK, 128), F32),
            pltpu.VMEM((FRAME, WIDTH), BF),
            pltpu.VMEM((2 * FRAME, 2 * WIDTH), BF),
            pltpu.VMEM((HEADS_HERE, HEAD_DIM, 2 * FRAME), BF),
            pltpu.VMEM((4 * HEADS_HERE, 2 * FRAME, PAIR), F32),
            pltpu.VMEM((2 * FRAME, WIDTH), F32),
            pltpu.VMEM((2 * FRAME, WIDTH), F32),
            pltpu.VMEM((FRAME, 2 * WIDTH), BF),
            pltpu.VMEM((FRAME, 2 * WIDTH), BF),
            pltpu.VMEM((FRAME, 3 * WIDTH), BF),
            pltpu.VMEM((PARTS, FRAME, COLS), BF),
            pltpu.VMEM((2 * PARTS, HALF, COLS), BF),
            pltpu.VMEM((2 * PARTS, HALF, COLS), BF),
            pltpu.VMEM((2 * PARTS, BLOCK, COLS), BF),
            pltpu.VMEM((2 * PARTS, BLOCK, COLS), BF),
            pltpu.VMEM((PARTS, BLOCK, COLS), BF),
            pltpu.VMEM((PARTS, BLOCK, COLS), BF),
            pltpu.VMEM((PAIR, WIDTH), BF),
            pltpu.VMEM((HEADS_HERE, 2 * FRAME, PAIR), BF),
            pltpu.VMEM((2 * PAIR, WIDTH), BF),
            pltpu.VMEM((2 * FRAME, 2 * PAIR), BF),
            pltpu.VMEM((2 * FRAME, 2 * PAIR), BF),
            pltpu.VMEM((BLOCK, D), F32),
            dma((5,)),
            dma((2, 32)),
            dma((2, 32)),
            dma((4,)),
            dma((4,)),
            dma((3,)),
            dma((3,)),
            dma((12 * PARTS,)),
            dma((12 * PARTS,)),
            dma((PARTS,)),
            dma((PARTS,)),
            pltpu.SemaphoreType.REGULAR,
            pltpu.SemaphoreType.REGULAR,
            pltpu.VMEM((PARTS, BLOCK, COLS), BF),
            dma((PARTS,)),
        ],
        compiler_params=pltpu.CompilerParams(
            collective_id=0, has_side_effects=True, vmem_limit_bytes=56 * 1024 * 1024
        ),
        name="frame_attention_grad",
    )(latents, cotangent, norm_gain.reshape(1, D), jnp.transpose(w_qkv, (1, 0, 2)), w_out)


def solution(mesh):
    return jax.shard_map(
        shards,
        mesh=mesh,
        in_specs=(
            P(("tm", "head"), None),
            P(("tm", "head"), None),
            P(),
            P(None, None, "head"),
            P("head", None),
        ),
        out_specs=P(("tm", "head"), None),
        check_vma=False,
    )
```
